256 devices in a mesh: wide: 16 (over y_lo, x, core), narrow: 16 (over z, y_hi).
Axes of the slice: x: 4, y: 4 (y_hi: 2, y_lo: 2; y = y_hi * 2 + y_lo), z: 8, core: 2. Of those that a mesh axis runs over, the one named last changes fastest.
Arguments:
- batch_index: int32 [1024], P('narrow'), may hold values from 0 to 255
- train_features: float32 [4096, 1024], P('narrow'), may hold values from -6 to 6
- train_labels: float32 [4096, 1000], P('narrow'), may hold values from -12 to 12
- centers: float32 [65536, 1024], P(('wide', 'narrow')), may hold values from -6 to 6
- weights: float32 [65536, 1000], P(('wide', 'narrow')), may hold values from -6 to 6
Outputs:
- new_weights: float32 [65536, 1000], P(('wide', 'narrow'))
- residual: float32 [1024, 1000], P('narrow')
The draws below stay inside these ranges and needn't reach their ends.
Inputs may be any that keep to these rules, and one draw needn't show every extreme that they name: `batch_index`: entry i names a row of the training shard held by narrow index i // 64.
All inputs are finite; a program needn't handle non-finite values.
Results may differ from the reference program's by a relative error of at most 0.0001.
Values sent between devices are 32-bit elements; how exact they have to be, the bound alone decides.
No kernel may reach another device: no remote copies, remote signals or barrier semaphores. Data moves between devices by JAX's collectives and lax.ppermute only.
A program may use at most 64 MiB of HBM per device.

```python
import math
import jax
import jax.numpy as jnp
from jax import lax

D = 1024
L = 1000
M_DEV = 256
BLOCK = 64
TRAIN_DEV = 256
BATCH = 1024
CENTERS = 65536
TRAIN = 4096
N_WIDE = 16
N_NARROW = 16


def shaped_rows(key, offset, row_count):
    own_key = jax.random.fold_in(key, offset)
    entry_key, norm_key = jax.random.split(own_key)
    sample = jax.random.normal(entry_key, (row_count, D), jnp.float32)
    square = jax.random.uniform(norm_key, (row_count, 1), jnp.float32, 0.85, 1.15)
    length = jnp.sqrt(jnp.sum(sample * sample, axis=1, keepdims=True))
    return jnp.clip(sample * jnp.sqrt(square * D) / length, -6.0, 6.0)


def draw_train_features(key, part):
    return shaped_rows(key, 11, TRAIN)


def draw_centers(key, part):
    return shaped_rows(key, 23, CENTERS)


def with_ends(values, rng, low, high):
    extent = values.shape
    index_at = [jax.random.randint(jax.random.fold_in(rng, axis), (), 0, extent[axis]) for axis in range(len(extent))]
    values = values.at[tuple(index_at)].set(low)
    longest = extent.index(max(extent))
    index_at[longest] = (index_at[longest] + 1) % extent[longest]
    return values.at[tuple(index_at)].set(high)


def shard_levels(rng, dims, shards, least, top_value):
    loudness = 1.0
    for position, blocks in shards:
        draws = jax.random.uniform(jax.random.fold_in(jax.random.fold_in(rng, 6), position), (blocks,), jnp.float32, least / len(shards), top_value / len(shards))
        loudness = loudness * jnp.repeat(jnp.exp(draws), dims[position] // blocks).reshape((-1,) + (1,) * (len(dims) - 1 - position))
    return loudness


def centred(key, dims, deviation, reach, shards=(), kind=jnp.bfloat16):
    drawn = jax.random.normal(key, dims, jnp.float32) * deviation
    if len(shards) > 0:
        drawn = shard_levels(key, dims, shards, -0.22, 0.18) * drawn
    return jnp.clip(drawn, min=-reach, max=reach).astype(kind)


def setup_inputs(seed: int = 0) -> dict:
    arg_keys = jax.random.split(jax.random.key(seed), 6)
    return {
        "batch_index": with_ends(jax.random.randint(arg_keys[0], (BATCH,), 0, TRAIN_DEV), jax.random.fold_in(arg_keys[0], 1), 0, TRAIN_DEV - 1).astype(jnp.int32),
        "train_features": draw_train_features(jax.random.fold_in(arg_keys[5], 71), 0),
        "train_labels": centred(arg_keys[2], (TRAIN, L), 2.0, 12.0, ((0, 16),), jnp.float32),
        "centers": draw_centers(jax.random.fold_in(arg_keys[5], 71), 0),
        "weights": centred(arg_keys[4], (CENTERS, L), 1.0, 6.0, ((0, 256),), jnp.float32),
    }


step_size = 1.0

def kernel_block(rows, centers_blk):
    inner = jnp.dot(rows, centers_blk.T, precision=lax.Precision.HIGHEST, preferred_element_type=jnp.float32)
    row_sq = lax.optimization_barrier(jnp.sum(rows * rows, axis=1))
    center_sq = lax.optimization_barrier(jnp.sum(centers_blk * centers_blk, axis=1))
    return jnp.exp((2.0 * rows.shape[1] - row_sq[:, None] - center_sq[None, :] + 2.0 * inner) / 128.0)

def reference(batch_index, train_features, train_labels, centers, weights):
    picks = jnp.arange(BATCH, dtype=jnp.int32) // BLOCK * TRAIN_DEV + batch_index.astype(jnp.int32)
    rows = jnp.take(train_features, picks, axis=0)
    targets = jnp.take(train_labels, picks, axis=0)
    groups = N_WIDE * N_NARROW
    center_blocks = centers.reshape(groups, M_DEV, D)
    weight_blocks = weights.reshape(groups, M_DEV, L)

    def accumulate(total, pair):
        kern = kernel_block(rows, pair[0])
        return (total + jnp.dot(kern, pair[1], precision=lax.Precision.HIGHEST, preferred_element_type=jnp.float32), None)
    partial_value, _ = lax.scan(accumulate, jnp.zeros((BATCH, L), jnp.float32), (center_blocks, weight_blocks))
    residual = partial_value * (1.0 / math.sqrt(CENTERS)) - targets

    def update(pair):
        kern = kernel_block(rows, pair[0])
        delta = lax.dot_general(kern, residual, (((0,), (0,)), ((), ())), precision=lax.Precision.HIGHEST, preferred_element_type=jnp.float32)
        return pair[1] - step_size / BATCH * delta
    new_weights = lax.map(update, (center_blocks, weight_blocks)).reshape(CENTERS, L)
    return (new_weights, residual)
```

```python
import math

import jax
import jax.numpy as jnp
from jax import lax
from jax.sharding import Mesh
from jax.sharding import PartitionSpec as P

AXES = ("y_lo", "x", "core", "z", "y_hi")
SIZES = (2, 4, 2, 8, 2)
WIDE_NARROW = AXES
NARROW = ("z", "y_hi")
PLANE = ("y_lo", "y_hi", "x")
SWAP = ((0, 1), (1, 0))

step_size = 1.0


def group_size(axes):
    return math.prod(lax.axis_size(axis) for axis in axes)


def exchange(array, axes):
    return lax.all_to_all(array, axes, 0, 0, tiled=True)


def spread(array, axes):
    count = group_size(axes)
    copies = jnp.broadcast_to(array[None], (count,) + array.shape)
    return exchange(copies.reshape((-1,) + array.shape[1:]), axes)


def scatter_sum(array, axes):
    count = group_size(axes)
    return exchange(array, axes).reshape((count, -1) + array.shape[1:]).sum(axis=0)


def pick(array, index):
    return array.at[index].get(mode="promise_in_bounds")


def per_device(batch_index, train_features, train_labels, centers, weights):
    block = batch_index.shape[0]
    features = centers.shape[1]
    outputs = weights.shape[1]
    wide = lax.axis_size("y_lo") * lax.axis_size("x") * lax.axis_size("core")
    devices = wide * group_size(NARROW)
    batch = block * group_size(NARROW)
    count = centers.shape[0] * devices
    scale = 1.0 / math.sqrt(count)
    core = lax.axis_index("core")
    own = block // wide
    start = (core * (wide // 2) + lax.axis_index(("y_lo", "x"))) * own
    index = lax.dynamic_slice_in_dim(batch_index, start, own, 0)
    rows = pick(train_features, index)
    targets = pick(train_labels, index)

    other_centers = lax.ppermute(centers, "core", SWAP)
    other_weights = lax.ppermute(weights, "core", SWAP)
    pair_centers = jnp.concatenate([centers, other_centers], axis=0)
    pair_weights = jnp.concatenate([weights, other_weights], axis=0)
    center_sq = jnp.sum(pair_centers * pair_centers, axis=1)

    rows_all = spread(spread(rows, ("z",)), PLANE)
    inner = lax.dot_general(
        rows_all,
        pair_centers,
        (((1,), (1,)), ((), ())),
        precision=lax.Precision.HIGH,
        preferred_element_type=jnp.float32,
    )
    row_sq = jnp.sum(rows_all * rows_all, axis=1)
    kernel = jnp.exp(
        (2.0 * features - row_sq[:, None] - center_sq[None, :] + 2.0 * inner) / 128.0
    )
    partial_value = jnp.dot(
        kernel, pair_weights, precision=lax.Precision.HIGH, preferred_element_type=jnp.float32
    )
    value = scatter_sum(scatter_sum(partial_value, PLANE), ("z",))
    resid = value * scale - targets
    resid_all = spread(spread(resid, ("z",)), PLANE)

    shaped = resid_all.reshape(
        lax.axis_size("y_lo"),
        lax.axis_size("y_hi"),
        lax.axis_size("x"),
        lax.axis_size("z"),
        own,
        outputs,
    )
    mine = lax.dynamic_index_in_dim(shaped, lax.axis_index("y_hi"), 1, keepdims=False)
    mine = lax.dynamic_index_in_dim(mine, lax.axis_index("z"), 2, keepdims=False)
    mine = mine.reshape(block // 2, outputs)
    theirs = lax.ppermute(mine, "core", SWAP)
    residual = jnp.where(
        core == 0,
        jnp.concatenate([mine, theirs], axis=0),
        jnp.concatenate([theirs, mine], axis=0),
    )
    delta = lax.dot_general(
        kernel,
        resid_all,
        (((0,), (0,)), ((), ())),
        precision=lax.Precision.HIGH,
        preferred_element_type=jnp.float32,
    )
    here = centers.shape[0]
    received = lax.ppermute(delta[here:], "core", SWAP)
    new_weights = weights - step_size / batch * (delta[:here] + received)
    return (new_weights, residual)


def solution(mesh):
    split = Mesh(mesh.devices.reshape(SIZES), AXES)
    placed = (
        P(NARROW),
        P(NARROW, None),
        P(NARROW, None),
        P(WIDE_NARROW, None),
        P(WIDE_NARROW, None),
    )
    return jax.shard_map(
        per_device,
        mesh=split,
        in_specs=placed,
        out_specs=(P(WIDE_NARROW, None), P(NARROW, None)),
        check_vma=False,
    )
```

```python
import math

import jax
import jax.numpy as jnp
from jax import lax
from jax.sharding import Mesh
from jax.sharding import PartitionSpec as P

AXES = ("y_lo", "x", "core", "z", "y_hi")
SIZES = (2, 4, 2, 8, 2)
WIDE_NARROW = AXES
NARROW = ("z", "y_hi")
PLANE = ("y_lo", "y_hi", "x")
SWAP = ((0, 1), (1, 0))
LANE = 128

step_size = 1.0


def group_size(axes):
    return math.prod(lax.axis_size(axis) for axis in axes)


def exchange(array, axes):
    return lax.all_to_all(array, axes, 0, 0, tiled=True)


def spread(array, axes):
    count = group_size(axes)
    copies = jnp.broadcast_to(array[None], (count,) + array.shape)
    return exchange(copies.reshape((-1,) + array.shape[1:]), axes)


def scatter_sum(array, axes):
    count = group_size(axes)
    return exchange(array, axes).reshape((count, -1) + array.shape[1:]).sum(axis=0)


def pick(array, index):
    return array.at[index].get(mode="promise_in_bounds")


def per_device(batch_index, train_features, train_labels, centers, weights):
    block = batch_index.shape[0]
    features = centers.shape[1]
    outputs = weights.shape[1]
    wide = lax.axis_size("y_lo") * lax.axis_size("x") * lax.axis_size("core")
    devices = wide * group_size(NARROW)
    batch = block * group_size(NARROW)
    count = centers.shape[0] * devices
    scale = 1.0 / math.sqrt(count)
    core = lax.axis_index("core")
    own = block // wide
    start = (core * (wide // 2) + lax.axis_index(("y_lo", "x"))) * own
    index = lax.dynamic_slice_in_dim(batch_index, start, own, 0)
    rows = pick(train_features, index)
    lanes = -(-outputs // LANE) * LANE
    fill = ((0, 0), (0, lanes - outputs))
    targets = jnp.pad(pick(train_labels, index), fill)

    other_centers = lax.ppermute(centers, "core", SWAP)
    other_weights = jnp.pad(lax.ppermute(weights, "core", SWAP), fill)
    own_weights = jnp.pad(weights, fill)

    rows_all = spread(spread(rows, ("z",)), PLANE)
    row_sq = jnp.sum(rows_all * rows_all, axis=1)

    def kernel_of(block_centers):
        inner = lax.dot_general(
            rows_all,
            block_centers,
            (((1,), (1,)), ((), ())),
            precision=lax.Precision.HIGH,
            preferred_element_type=jnp.float32,
        )
        center_sq = jnp.sum(block_centers * block_centers, axis=1)
        return jnp.exp(
            (2.0 * features - row_sq[:, None] - center_sq[None, :] + 2.0 * inner) / 128.0
        )

    def product(kernel, block_weights):
        return jnp.dot(
            kernel,
            block_weights,
            precision=lax.Precision.HIGH,
            preferred_element_type=jnp.float32,
        )

    own_kernel = kernel_of(centers)
    other_kernel = kernel_of(other_centers)
    partial_value = product(own_kernel, own_weights) + product(other_kernel, other_weights)
    value = scatter_sum(scatter_sum(partial_value, PLANE), ("z",))
    resid = value * scale - targets
    resid_all = spread(spread(resid, ("z",)), PLANE)

    def delta_of(kernel):
        return lax.dot_general(
            resid_all,
            kernel,
            (((0,), (0,)), ((), ())),
            precision=lax.Precision.HIGH,
            preferred_element_type=jnp.float32,
        )[:outputs]

    received = lax.ppermute(delta_of(other_kernel), "core", SWAP)
    delta = delta_of(own_kernel)
    new_weights = weights - step_size / batch * (delta + received).T

    plane = own * lax.axis_size("z")
    place = lax.axis_index("z") * own + lax.axis_index("y_hi") * lax.axis_size("x") * plane
    mine = jnp.concatenate(
        [
            lax.dynamic_slice_in_dim(
                resid_all, place + (y * lax.axis_size("y_hi") * lax.axis_size("x") + x) * plane, own, 0
            )
            for y in range(lax.axis_size("y_lo"))
            for x in range(lax.axis_size("x"))
        ],
        axis=0,
    )[:, :outputs]
    theirs = lax.ppermute(mine, "core", SWAP)
    residual = jnp.where(
        core == 0,
        jnp.concatenate([mine, theirs], axis=0),
        jnp.concatenate([theirs, mine], axis=0),
    )
    return (new_weights, residual)


def solution(mesh):
    split = Mesh(mesh.devices.reshape(SIZES), AXES)
    placed = (
        P(NARROW),
        P(NARROW, None),
        P(NARROW, None),
        P(WIDE_NARROW, None),
        P(WIDE_NARROW, None),
    )
    return jax.shard_map(
        per_device,
        mesh=split,
        in_specs=placed,
        out_specs=(P(WIDE_NARROW, None), P(NARROW, None)),
        check_vma=False,
    )
```

```python
import math

import jax
import jax.numpy as jnp
from jax import lax
from jax.sharding import Mesh
from jax.sharding import PartitionSpec as P

AXES = ("y_lo", "x", "core", "z", "y_hi")
SIZES = (2, 4, 2, 8, 2)
WIDE_NARROW = AXES
NARROW = ("z", "y_hi")
RING = 4
LEVELS = 8
LANE = 128
ORDER = (2, 1, 3)

step_size = 1.0


def position(x, y, z, core):
    x, y = x % RING, y % RING
    return (((y % 2 * RING + x) * 2 + core) * LEVELS + z) * 2 + y // 2


def everywhere():
    return [
        (x, y, z, core)
        for x in range(RING)
        for y in range(RING)
        for z in range(LEVELS)
        for core in range(2)
    ]


def bulk_shift(offset):
    return [
        (
            position(x, y, z, core),
            position(x + offset, y, z, 0) if core == 0 else position(x, y + offset, z, 1),
        )
        for x, y, z, core in everywhere()
    ]


SWAP = [(position(x, y, z, core), position(x, y, z, 1 - core)) for x, y, z, core in everywhere()]
COLUMNS = [
    [position(x, y, z, core) for z in range(LEVELS)]
    for x in range(RING)
    for y in range(RING)
    for core in range(2)
]
RINGS = [
    [position(i, k, z, 0) if core == 0 else position(k, i, z, 1) for k in range(RING)]
    for i in range(RING)
    for z in range(LEVELS)
    for core in range(2)
]


def permute(array, pairs):
    return lax.ppermute(array, AXES, pairs)


def exchange(array, groups):
    return lax.all_to_all(array, AXES, 0, 0, axis_index_groups=groups, tiled=True)


def spread(array, groups):
    count = len(groups[0])
    copies = jnp.broadcast_to(array[None], (count,) + array.shape)
    return exchange(copies.reshape((-1,) + array.shape[1:]), groups)


def scatter_sum(array, groups):
    count = len(groups[0])
    return exchange(array, groups).reshape((count, -1) + array.shape[1:]).sum(axis=0)


def quarters(own):
    received = {offset: permute(own, bulk_shift(-offset)) for offset in ORDER}
    received[0] = own
    return received


def pick(array, index):
    return array.at[index].get(mode="promise_in_bounds")


def dot(left, right, contract):
    return lax.dot_general(
        left,
        right,
        (contract, ((), ())),
        precision=lax.Precision.HIGH,
        preferred_element_type=jnp.float32,
    )


def per_device(batch_index, train_features, train_labels, centers, weights):
    block = batch_index.shape[0]
    features = centers.shape[1]
    outputs = weights.shape[1]
    here = centers.shape[0]
    devices = math.prod(SIZES)
    batch = block * LEVELS * 2
    scale = 1.0 / math.sqrt(here * devices)
    x, core, z = lax.axis_index("x"), lax.axis_index("core"), lax.axis_index("z")
    y_lo, y_hi = lax.axis_index("y_lo"), lax.axis_index("y_hi")
    y = y_hi * 2 + y_lo
    own = block // (2 * RING * 2)
    start = (core * 2 * RING + y_lo * RING + x) * own
    index = lax.dynamic_slice_in_dim(batch_index, start, own, 0)
    rows = pick(train_features, index)
    lanes = -(-outputs // LANE) * LANE
    fill = ((0, 0), (0, lanes - outputs))
    targets = jnp.pad(pick(train_labels, index), fill)

    pair_centers = jnp.concatenate([centers, permute(centers, SWAP)], axis=0)
    pair_weights = jnp.pad(jnp.concatenate([weights, permute(weights, SWAP)], axis=0), fill)
    center_sq = jnp.sum(pair_centers * pair_centers, axis=1)

    rows_of = quarters(spread(spread(rows, COLUMNS), RINGS))
    kernel_of = {}
    for offset, part in rows_of.items():
        row_sq = jnp.sum(part * part, axis=1)
        inner = dot(part, pair_centers, ((1,), (1,)))
        kernel_of[offset] = jnp.exp(
            (2.0 * features - row_sq[:, None] - center_sq[None, :] + 2.0 * inner) / 128.0
        )
    value = dot(kernel_of[0], pair_weights, ((1,), (0,)))
    for offset in ORDER:
        value = value + permute(
            dot(kernel_of[offset], pair_weights, ((1,), (0,))), bulk_shift(offset)
        )
    value = scatter_sum(scatter_sum(value, RINGS), COLUMNS)
    resid_of = quarters(spread(spread(value * scale - targets, COLUMNS), RINGS))

    def delta_of(low, high):
        return sum(
            dot(resid_of[offset], kernel_of[offset][:, low:high], ((0,), (0,)))
            for offset in (0,) + ORDER
        )[:outputs]

    received = permute(delta_of(here, 2 * here), SWAP)
    delta = delta_of(0, here)
    new_weights = weights - step_size / batch * (delta + received).T

    quarter = RING * LEVELS * own
    resid_all = jnp.concatenate([resid_of[offset] for offset in range(RING)], axis=0)
    pieces = []
    for low in range(2):
        for column in range(RING):
            line = y_hi * 2 + low
            offset = jnp.where(core == 0, column - x, line - y) % RING
            slot = jnp.where(core == 0, line, column)
            place = offset * quarter + (slot * LEVELS + z) * own
            pieces.append(lax.dynamic_slice_in_dim(resid_all, place, own, 0))
    mine = jnp.concatenate(pieces, axis=0)[:, :outputs]
    theirs = permute(mine, SWAP)
    residual = jnp.where(
        core == 0,
        jnp.concatenate([mine, theirs], axis=0),
        jnp.concatenate([theirs, mine], axis=0),
    )
    return (new_weights, residual)


def solution(mesh):
    split = Mesh(mesh.devices.reshape(SIZES), AXES)
    placed = (
        P(NARROW),
        P(NARROW, None),
        P(NARROW, None),
        P(WIDE_NARROW, None),
        P(WIDE_NARROW, None),
    )
    return jax.shard_map(
        per_device,
        mesh=split,
        in_specs=placed,
        out_specs=(P(WIDE_NARROW, None), P(NARROW, None)),
        check_vma=False,
    )
```

```python
import math

import jax
import jax.numpy as jnp
from jax import lax
from jax.sharding import Mesh
from jax.sharding import PartitionSpec as P

AXES = ("y_lo", "x", "core", "z", "y_hi")
SIZES = (2, 4, 2, 8, 2)
WIDE_NARROW = AXES
NARROW = ("z", "y_hi")
RING = 4
LEVELS = 8
LANE = 128
ORDER = (2, 1, 3)

step_size = 1.0


def position(x, y, z, core):
    x, y = x % RING, y % RING
    return (((y % 2 * RING + x) * 2 + core) * LEVELS + z) * 2 + y // 2


def everywhere():
    return [
        (x, y, z, core)
        for x in range(RING)
        for y in range(RING)
        for z in range(LEVELS)
        for core in range(2)
    ]


def bulk_shift(offset):
    return [
        (
            position(x, y, z, core),
            position(x + offset, y, z, 0) if core == 0 else position(x, y + offset, z, 1),
        )
        for x, y, z, core in everywhere()
    ]


SWAP = [(position(x, y, z, core), position(x, y, z, 1 - core)) for x, y, z, core in everywhere()]
SHEETS = [
    [
        position(i, k, z, 0) if core == 0 else position(k, i, z, 1)
        for k in range(RING)
        for z in range(LEVELS)
    ]
    for i in range(RING)
    for core in range(2)
]


def permute(array, pairs):
    return lax.ppermute(array, AXES, pairs)


def exchange(array, groups):
    return lax.all_to_all(array, AXES, 0, 0, axis_index_groups=groups, tiled=True)


def spread(array, groups):
    count = len(groups[0])
    copies = jnp.broadcast_to(array[None], (count,) + array.shape)
    return exchange(copies.reshape((-1,) + array.shape[1:]), groups)


def scatter_sum(array, groups):
    count = len(groups[0])
    return exchange(array, groups).reshape((count, -1) + array.shape[1:]).sum(axis=0)


def quarters(own):
    received = {offset: permute(own, bulk_shift(-offset)) for offset in ORDER}
    received[0] = own
    return received


def pick(array, index):
    return array.at[index].get(mode="promise_in_bounds")


def dot(left, right, contract):
    return lax.dot_general(
        left,
        right,
        (contract, ((), ())),
        precision=lax.Precision.HIGH,
        preferred_element_type=jnp.float32,
    )


def per_device(batch_index, train_features, train_labels, centers, weights):
    block = batch_index.shape[0]
    features = centers.shape[1]
    outputs = weights.shape[1]
    here = centers.shape[0]
    devices = math.prod(SIZES)
    batch = block * LEVELS * 2
    scale = 1.0 / math.sqrt(here * devices)
    x, core, z = lax.axis_index("x"), lax.axis_index("core"), lax.axis_index("z")
    y_lo, y_hi = lax.axis_index("y_lo"), lax.axis_index("y_hi")
    y = y_hi * 2 + y_lo
    own = block // (2 * RING * 2)
    start = (core * 2 * RING + y_lo * RING + x) * own
    index = lax.dynamic_slice_in_dim(batch_index, start, own, 0)
    rows = pick(train_features, index)
    lanes = -(-outputs // LANE) * LANE
    fill = ((0, 0), (0, lanes - outputs))
    targets = jnp.pad(pick(train_labels, index), fill)

    pair_centers = jnp.concatenate([centers, permute(centers, SWAP)], axis=0)
    pair_weights = jnp.pad(jnp.concatenate([weights, permute(weights, SWAP)], axis=0), fill)
    pair_centers, pair_weights = lax.optimization_barrier((pair_centers, pair_weights))
    center_sq = jnp.sum(pair_centers * pair_centers, axis=1)

    def kernel_of(part):
        row_sq = jnp.sum(part * part, axis=1)
        inner = dot(part, pair_centers, ((1,), (1,)))
        kernel = jnp.exp(
            (2.0 * features - row_sq[:, None] - center_sq[None, :] + 2.0 * inner) / 128.0
        )
        return lax.optimization_barrier(kernel)

    rows_of = quarters(spread(rows, SHEETS))
    kernels = {0: kernel_of(rows_of[0])}
    value = dot(kernels[0], pair_weights, ((1,), (0,)))
    later = [rows_of[offset] for offset in ORDER]
    *later, value = lax.optimization_barrier((*later, value))
    for offset, part in zip(ORDER, later):
        kernels[offset] = kernel_of(part)
        value = value + permute(
            dot(kernels[offset], pair_weights, ((1,), (0,))), bulk_shift(offset)
        )
    value = scatter_sum(value, SHEETS)
    resid_of = quarters(spread(value * scale - targets, SHEETS))
    resid_all = jnp.concatenate([resid_of[offset] for offset in range(RING)], axis=0)
    kernel_all = jnp.concatenate([kernels[offset] for offset in range(RING)], axis=0)
    resid_all, kernel_all = lax.optimization_barrier((resid_all, kernel_all))

    received = permute(dot(resid_all, kernel_all[:, here:], ((0,), (0,)))[:outputs], SWAP)
    delta = dot(resid_all, kernel_all[:, :here], ((0,), (0,)))[:outputs]
    new_weights = weights - step_size / batch * (delta + received).T

    quarter = RING * LEVELS * own
    pieces = []
    for low in range(2):
        for column in range(RING):
            line = y_hi * 2 + low
            offset = jnp.where(core == 0, column - x, line - y) % RING
            slot = jnp.where(core == 0, line, column)
            place = offset * quarter + (slot * LEVELS + z) * own
            pieces.append(lax.dynamic_slice_in_dim(resid_all, place, own, 0))
    mine = jnp.concatenate(pieces, axis=0)[:, :outputs]
    theirs = permute(mine, SWAP)
    residual = jnp.where(
        core == 0,
        jnp.concatenate([mine, theirs], axis=0),
        jnp.concatenate([theirs, mine], axis=0),
    )
    return (new_weights, residual)


def solution(mesh):
    split = Mesh(mesh.devices.reshape(SIZES), AXES)
    placed = (
        P(NARROW),
        P(NARROW, None),
        P(NARROW, None),
        P(WIDE_NARROW, None),
        P(WIDE_NARROW, None),
    )
    return jax.shard_map(
        per_device,
        mesh=split,
        in_specs=placed,
        out_specs=(P(WIDE_NARROW, None), P(NARROW, None)),
        check_vma=False,
    )
```

```python
import math

import jax
import jax.numpy as jnp
from jax import lax
from jax.experimental import pallas as pl
from jax.experimental.pallas import tpu as pltpu
from jax.sharding import Mesh
from jax.sharding import PartitionSpec as P

AXES = ("y_lo", "x", "core", "z", "y_hi")
SIZES = (2, 4, 2, 8, 2)
WIDE_NARROW = AXES
NARROW = ("z", "y_hi")
RING = 4
LEVELS = 8
LANE = 128
ORDER = (2, 1, 3)

VMEM_BYTES = 24 * 1024 * 1024

step_size = 1.0


def position(x, y, z, core):
    x, y = x % RING, y % RING
    return (((y % 2 * RING + x) * 2 + core) * LEVELS + z) * 2 + y // 2


def everywhere():
    return [
        (x, y, z, core)
        for x in range(RING)
        for y in range(RING)
        for z in range(LEVELS)
        for core in range(2)
    ]


def bulk_shift(offset):
    return [
        (
            position(x, y, z, core),
            position(x + offset, y, z, 0) if core == 0 else position(x, y + offset, z, 1),
        )
        for x, y, z, core in everywhere()
    ]


SWAP = [(position(x, y, z, core), position(x, y, z, 1 - core)) for x, y, z, core in everywhere()]
SHEETS = [
    [
        position(i, k, z, 0) if core == 0 else position(k, i, z, 1)
        for k in range(RING)
        for z in range(LEVELS)
    ]
    for i in range(RING)
    for core in range(2)
]


def permute(array, pairs):
    return lax.ppermute(array, AXES, pairs)


def exchange(array, groups):
    return lax.all_to_all(array, AXES, 0, 0, axis_index_groups=groups, tiled=True)


def spread(array, groups):
    count = len(groups[0])
    copies = jnp.broadcast_to(array[None], (count,) + array.shape)
    return exchange(copies.reshape((-1,) + array.shape[1:]), groups)


def scatter_sum(array, groups):
    count = len(groups[0])
    return exchange(array, groups).reshape((count, -1) + array.shape[1:]).sum(axis=0)


def quarters(own):
    received = {offset: permute(own, bulk_shift(-offset)) for offset in ORDER}
    received[0] = own
    return received


def pick(array, index):
    return array.at[index].get(mode="promise_in_bounds")


def parts(array):
    high = array.astype(jnp.bfloat16)
    return high, (array - high.astype(jnp.float32)).astype(jnp.bfloat16)


def rounded_parts(array):
    high = lax.reduce_precision(array, 8, 7)
    return high.astype(jnp.bfloat16), (array - high).astype(jnp.bfloat16)


def product(left, right, contract):
    def one(a, b):
        return lax.dot_general(
            a, b, (contract, ((), ())), preferred_element_type=jnp.float32
        )

    return one(left[0], right[0]) + (one(left[0], right[1]) + one(left[1], right[0]))


def quarter_kernel(
    rows, centers_high, centers_low, center_sq, weights_high, weights_low, value, high, low
):
    features = rows.shape[1]
    part = rows[...]
    row_sq = jnp.sum(part * part, axis=1, keepdims=True)
    inner = product(parts(part), (centers_high[...], centers_low[...]), ((1,), (0,)))
    kernel = parts(jnp.exp((2.0 * features - row_sq - center_sq[...] + 2.0 * inner) / 128.0))
    high[...], low[...] = kernel
    value[...] = product(kernel, (weights_high[...], weights_low[...]), ((1,), (0,)))


def first_delta_kernel(resid_0, resid_1, resid_2, resid_3, high, low, delta, out_high, out_low):
    quarter = resid_0.shape[0]
    for i, resid in enumerate((resid_0, resid_1, resid_2, resid_3)):
        place = pl.ds(i * quarter, quarter)
        out_high[place, :], out_low[place, :] = parts(resid[...])
    found = product((high[...], low[...]), (out_high[...], out_low[...]), ((0,), (0,)))
    delta[...] = found.T[: delta.shape[0]]


def second_delta_kernel(resid_high, resid_low, high, low, delta):
    found = product((high[...], low[...]), (resid_high[...], resid_low[...]), ((0,), (0,)))
    delta[...] = found.T[: delta.shape[0]]


def call(kernel, outs, *operands):
    return pl.pallas_call(
        kernel,
        out_shape=[jax.ShapeDtypeStruct(shape, dtype) for shape, dtype in outs],
        compiler_params=pltpu.CompilerParams(vmem_limit_bytes=VMEM_BYTES),
    )(*operands)


def per_device(batch_index, train_features, train_labels, centers, weights):
    block = batch_index.shape[0]
    features = centers.shape[1]
    outputs = weights.shape[1]
    here = centers.shape[0]
    devices = math.prod(SIZES)
    batch = block * LEVELS * 2
    scale = 1.0 / math.sqrt(here * devices)
    x, core, z = lax.axis_index("x"), lax.axis_index("core"), lax.axis_index("z")
    y_lo, y_hi = lax.axis_index("y_lo"), lax.axis_index("y_hi")
    y = y_hi * 2 + y_lo
    own = block // (2 * RING * 2)
    start = (core * 2 * RING + y_lo * RING + x) * own
    index = lax.dynamic_slice_in_dim(batch_index, start, own, 0)
    rows = pick(train_features, index)
    lanes = -(-outputs // LANE) * LANE
    fill = ((0, 0), (0, lanes - outputs))
    targets = jnp.pad(pick(train_labels, index), fill)

    pair_centers = jnp.concatenate([centers, permute(centers, SWAP)], axis=0)
    pair_weights = jnp.pad(jnp.concatenate([weights, permute(weights, SWAP)], axis=0), fill)
    held = lax.optimization_barrier(
        (
            *rounded_parts(pair_centers.T),
            jnp.sum(pair_centers * pair_centers, axis=1)[None, :],
            *rounded_parts(pair_weights),
        )
    )
    quarter = RING * LEVELS * own
    pair = 2 * here

    def quarter_of(part):
        return call(
            quarter_kernel,
            (
                ((quarter, lanes), jnp.float32),
                ((quarter, pair), jnp.bfloat16),
                ((quarter, pair), jnp.bfloat16),
            ),
            part,
            *held,
        )

    rows_of = quarters(spread(rows, SHEETS))
    done = {0: quarter_of(rows_of[0])}
    value = done[0][0]
    later = [rows_of[offset] for offset in ORDER]
    *later, value = lax.optimization_barrier((*later, value))
    for offset, part in zip(ORDER, later):
        done[offset] = quarter_of(part)
        value = value + permute(done[offset][0], bulk_shift(offset))
    high = jnp.concatenate([done[offset][1] for offset in range(RING)], axis=0)
    low = jnp.concatenate([done[offset][2] for offset in range(RING)], axis=0)
    value = scatter_sum(value, SHEETS)
    resid_of = quarters(spread(value * scale - targets, SHEETS))
    resid_list = [resid_of[offset] for offset in range(RING)]

    batch_rows = RING * quarter
    first, resid_high, resid_low = call(
        first_delta_kernel,
        (
            ((outputs, here), jnp.float32),
            ((batch_rows, lanes), jnp.bfloat16),
            ((batch_rows, lanes), jnp.bfloat16),
        ),
        *resid_list,
        high[:, here:],
        low[:, here:],
    )
    received = permute(first, SWAP)
    (second,) = call(
        second_delta_kernel,
        (((outputs, here), jnp.float32),),
        resid_high,
        resid_low,
        high[:, :here],
        low[:, :here],
    )
    new_weights = (weights.T - step_size / batch * (second + received)).T

    *resid_list, _ = lax.optimization_barrier((*resid_list, first))
    resid_all = jnp.concatenate(resid_list, axis=0)
    pieces = []
    for low in range(2):
        for column in range(RING):
            line = y_hi * 2 + low
            offset = jnp.where(core == 0, column - x, line - y) % RING
            slot = jnp.where(core == 0, line, column)
            place = offset * quarter + (slot * LEVELS + z) * own
            pieces.append(lax.dynamic_slice_in_dim(resid_all, place, own, 0))
    mine = jnp.concatenate(pieces, axis=0)[:, :outputs]
    theirs = permute(mine, SWAP)
    residual = jnp.where(
        core == 0,
        jnp.concatenate([mine, theirs], axis=0),
        jnp.concatenate([theirs, mine], axis=0),
    )
    return (new_weights, residual)


def solution(mesh):
    split = Mesh(mesh.devices.reshape(SIZES), AXES)
    placed = (
        P(NARROW),
        P(NARROW, None),
        P(NARROW, None),
        P(WIDE_NARROW, None),
        P(WIDE_NARROW, None),
    )
    return jax.shard_map(
        per_device,
        mesh=split,
        in_specs=placed,
        out_specs=(P(WIDE_NARROW, None), P(NARROW, None)),
        check_vma=False,
    )
```

```python
import math

import jax
import jax.numpy as jnp
from jax import lax
from jax.experimental import pallas as pl
from jax.experimental.pallas import tpu as pltpu
from jax.sharding import Mesh
from jax.sharding import PartitionSpec as P

AXES = ("y_lo", "x", "core", "z", "y_hi")
SIZES = (2, 4, 2, 8, 2)
WIDE_NARROW = AXES
NARROW = ("z", "y_hi")
RING = 4
LEVELS = 8
LANE = 128
ORDER = (2, 1, 3)

VMEM_BYTES = 24 * 1024 * 1024

step_size = 1.0


def position(x, y, z, core):
    x, y = x % RING, y % RING
    return (((y % 2 * RING + x) * 2 + core) * LEVELS + z) * 2 + y // 2


def everywhere():
    return [
        (x, y, z, core)
        for x in range(RING)
        for y in range(RING)
        for z in range(LEVELS)
        for core in range(2)
    ]


def bulk_shift(offset):
    return [
        (
            position(x, y, z, core),
            position(x + offset, y, z, 0) if core == 0 else position(x, y + offset, z, 1),
        )
        for x, y, z, core in everywhere()
    ]


def ring_shift(offset):
    return [
        (
            position(x, y, z, core),
            position(x, y + offset, z, 0) if core == 0 else position(x + offset, y, z, 1),
        )
        for x, y, z, core in everywhere()
    ]


SWAP = [(position(x, y, z, core), position(x, y, z, 1 - core)) for x, y, z, core in everywhere()]
COLUMNS = [
    [position(x, y, z, core) for z in range(LEVELS)]
    for x in range(RING)
    for y in range(RING)
    for core in range(2)
]


def permute(array, pairs):
    return lax.ppermute(array, AXES, pairs)


def exchange(array, groups):
    return lax.all_to_all(array, AXES, 0, 0, axis_index_groups=groups, tiled=True)


def spread(array, groups):
    count = len(groups[0])
    copies = jnp.broadcast_to(array[None], (count,) + array.shape)
    return exchange(copies.reshape((-1,) + array.shape[1:]), groups)


def scatter_sum(array, groups):
    count = len(groups[0])
    return exchange(array, groups).reshape((count, -1) + array.shape[1:]).sum(axis=0)


def gathered(own, shift):
    received = {offset: permute(own, shift(-offset)) for offset in ORDER}
    received[0] = own
    return received


def quarters(column):
    pieces = gathered(column, ring_shift)
    quarter = jnp.concatenate([pieces[offset] for offset in range(RING)], axis=0)
    return gathered(quarter, bulk_shift)


def ring_sum(array):
    pieces = jnp.split(array, RING, axis=0)
    total = pieces[0]
    for offset in ORDER:
        total = total + permute(pieces[offset], ring_shift(offset))
    return total


def pick(array, index):
    return array.at[index].get(mode="promise_in_bounds")


def parts(array):
    high = array.astype(jnp.bfloat16)
    return high, (array - high.astype(jnp.float32)).astype(jnp.bfloat16)


def product(left, right, contract):
    def one(a, b):
        return lax.dot_general(
            a, b, (contract, ((), ())), preferred_element_type=jnp.float32
        )

    return one(left[0], right[0]) + (one(left[0], right[1]) + one(left[1], right[0]))


def prepare_kernel(
    own_centers, other_centers, own_weights, other_weights, high, low, center_sq, value_high, value_low
):
    here = own_centers.shape[0]
    outputs, lanes = own_weights.shape[0], value_high.shape[1]
    for i, (centers, weights) in enumerate(
        ((own_centers, own_weights), (other_centers, other_weights))
    ):
        place = pl.ds(i * here, here)
        turned = centers[...].T
        center_sq[:, place] = jnp.sum(turned * turned, axis=0, keepdims=True)
        high[:, place], low[:, place] = parts(turned)
        zeros = jnp.zeros((lanes - outputs, here), jnp.float32)
        padded = jnp.concatenate([weights[...], zeros], axis=0)
        value_high[place, :], value_low[place, :] = parts(padded.T)


def quarter_kernel(
    rows, centers_high, centers_low, center_sq, weights_high, weights_low, value, high, low
):
    features = rows.shape[1]
    part = rows[...]
    row_sq = jnp.sum(part * part, axis=1, keepdims=True)
    inner = product(parts(part), (centers_high[...], centers_low[...]), ((1,), (0,)))
    kernel = parts(jnp.exp((2.0 * features - row_sq - center_sq[...] + 2.0 * inner) / 128.0))
    high[...], low[...] = kernel
    value[...] = product(kernel, (weights_high[...], weights_low[...]), ((1,), (0,)))


def delta_kernel(resid_0, resid_1, resid_2, resid_3, high, low, delta, resid_high, resid_low):
    quarter = resid_0.shape[0]
    for i, resid in enumerate((resid_0, resid_1, resid_2, resid_3)):
        place = pl.ds(i * quarter, quarter)
        resid_high[place, :], resid_low[place, :] = parts(resid[...])
    found = product((high[...], low[...]), (resid_high[...], resid_low[...]), ((0,), (0,)))
    delta[...] = found.T[: delta.shape[0]]


def call(kernel, outs, *operands, scratch=()):
    return pl.pallas_call(
        kernel,
        out_shape=[jax.ShapeDtypeStruct(shape, dtype) for shape, dtype in outs],
        scratch_shapes=[pltpu.VMEM(shape, dtype) for shape, dtype in scratch],
        compiler_params=pltpu.CompilerParams(vmem_limit_bytes=VMEM_BYTES),
    )(*operands)


def per_device(batch_index, train_features, train_labels, centers, weights):
    block = batch_index.shape[0]
    features = centers.shape[1]
    outputs = weights.shape[1]
    here = centers.shape[0]
    devices = math.prod(SIZES)
    batch = block * LEVELS * 2
    scale = 1.0 / math.sqrt(here * devices)
    x, core, z = lax.axis_index("x"), lax.axis_index("core"), lax.axis_index("z")
    y_lo, y_hi = lax.axis_index("y_lo"), lax.axis_index("y_hi")
    y = y_hi * 2 + y_lo
    own = block // (2 * RING * 2)
    start = (core * 2 * RING + y_lo * RING + x) * own
    index = lax.dynamic_slice_in_dim(batch_index, start, own, 0)
    rows = pick(train_features, index)
    lanes = -(-outputs // LANE) * LANE
    fill = ((0, 0), (0, lanes - outputs))
    targets = jnp.pad(pick(train_labels, index), fill)

    column, centers, own_weights = lax.optimization_barrier(
        (spread(rows, COLUMNS), centers, weights)
    )
    quarter = RING * LEVELS * own
    pair = 2 * here
    held = call(
        prepare_kernel,
        (
            ((features, pair), jnp.bfloat16),
            ((features, pair), jnp.bfloat16),
            ((1, pair), jnp.float32),
            ((pair, lanes), jnp.bfloat16),
            ((pair, lanes), jnp.bfloat16),
        ),
        centers,
        permute(centers, SWAP),
        own_weights.T,
        permute(own_weights, SWAP).T,
    )

    def quarter_of(part):
        return call(
            quarter_kernel,
            (
                ((quarter, lanes), jnp.float32),
                ((quarter, pair), jnp.bfloat16),
                ((quarter, pair), jnp.bfloat16),
            ),
            part,
            *held,
        )

    rows_of = quarters(column)
    done = {0: quarter_of(rows_of[0])}
    value = done[0][0]
    later = [rows_of[offset] for offset in ORDER]
    *later, value = lax.optimization_barrier((*later, value))
    for offset, part in zip(ORDER, later):
        done[offset] = quarter_of(part)
        value = value + permute(done[offset][0], bulk_shift(offset))
    high = jnp.concatenate([done[offset][1] for offset in range(RING)], axis=0)
    low = jnp.concatenate([done[offset][2] for offset in range(RING)], axis=0)
    value = scatter_sum(ring_sum(value), COLUMNS)
    resid_of = quarters(spread(value * scale - targets, COLUMNS))
    resid_list = [resid_of[offset] for offset in range(RING)]

    def delta_of(resid, low_end, high_end):
        return call(
            delta_kernel,
            (((outputs, here), jnp.float32),),
            *resid,
            high[:, low_end:high_end],
            low[:, low_end:high_end],
            scratch=(((RING * quarter, lanes), jnp.bfloat16),) * 2,
        )[0]

    first = delta_of(resid_list, here, pair)
    received = permute(first, SWAP)
    *resid_list, first = lax.optimization_barrier((*resid_list, first))
    second = delta_of(resid_list, 0, here)
    new_weights = (weights.T - step_size / batch * (second + received)).T

    resid_all = jnp.concatenate(resid_list, axis=0)
    pieces = []
    for low in range(2):
        for column in range(RING):
            line = y_hi * 2 + low
            offset = jnp.where(core == 0, column - x, line - y) % RING
            slot = jnp.where(core == 0, line, column)
            turn = (slot - jnp.where(core == 0, y, x)) % RING
            place = offset * quarter + (turn * LEVELS + z) * own
            pieces.append(lax.dynamic_slice_in_dim(resid_all, place, own, 0))
    mine = jnp.concatenate(pieces, axis=0)[:, :outputs]
    theirs = permute(mine, SWAP)
    residual = jnp.where(
        core == 0,
        jnp.concatenate([mine, theirs], axis=0),
        jnp.concatenate([theirs, mine], axis=0),
    )
    return (new_weights, residual)


def solution(mesh):
    split = Mesh(mesh.devices.reshape(SIZES), AXES)
    placed = (
        P(NARROW),
        P(NARROW, None),
        P(NARROW, None),
        P(WIDE_NARROW, None),
        P(WIDE_NARROW, None),
    )
    return jax.shard_map(
        per_device,
        mesh=split,
        in_specs=placed,
        out_specs=(P(WIDE_NARROW, None), P(NARROW, None)),
        check_vma=False,
    )
```

```python
import math

import jax
import jax.numpy as jnp
from jax import lax
from jax.experimental import pallas as pl
from jax.experimental.pallas import tpu as pltpu
from jax.sharding import Mesh
from jax.sharding import PartitionSpec as P

AXES = ("y_lo", "x", "core", "z", "y_hi")
SIZES = (2, 4, 2, 8, 2)
WIDE_NARROW = AXES
NARROW = ("z", "y_hi")
RING = 4
LEVELS = 8
LANE = 128
WAYS = (1, 2, 3)

VMEM_BYTES = 16 * 1024 * 1024

step_size = 1.0


def position(x, y, z, core):
    x, y = x % RING, y % RING
    return (((y % 2 * RING + x) * 2 + core) * LEVELS + z) * 2 + y // 2


def everywhere():
    return [
        (x, y, z, core)
        for x in range(RING)
        for y in range(RING)
        for z in range(LEVELS)
        for core in range(2)
    ]


def beside(place, core):
    return place + 1 if place % 2 == core else place - 1


def neighbour(x, y, z, core, way):
    if way == 1:
        x = beside(x, core)
    elif way == 2:
        y = beside(y, core)
    elif way == 3:
        z = beside(z, core)
    return position(x, y, z % LEVELS, core)


def swap_pairs(way):
    return [(position(*device), neighbour(*device, way)) for device in everywhere()]


SWAP = [(position(x, y, z, core), position(x, y, z, 1 - core)) for x, y, z, core in everywhere()]
CLASSES = [
    [
        position(2 * i + (low + z) % 2, 2 * k + (high + z) % 2, z, core)
        for i in range(RING // 2)
        for k in range(RING // 2)
        for z in range(LEVELS)
    ]
    for low in range(2)
    for high in range(2)
    for core in range(2)
]


def permute(array, pairs):
    return lax.ppermute(array, AXES, pairs)


def exchange(array, groups):
    return lax.all_to_all(array, AXES, 0, 0, axis_index_groups=groups, tiled=True)


def spread(array, groups):
    count = len(groups[0])
    copies = jnp.broadcast_to(array[None], (count,) + array.shape)
    return exchange(copies.reshape((-1,) + array.shape[1:]), groups)


def scatter_sum(array, groups):
    count = len(groups[0])
    return exchange(array, groups).reshape((count, -1) + array.shape[1:]).sum(axis=0)


def quarters(own):
    received = {way: permute(own, swap_pairs(way)) for way in WAYS}
    received[0] = own
    return received


def pick(array, index):
    return array.at[index].get(mode="promise_in_bounds")


def parts(array):
    high = array.astype(jnp.bfloat16)
    return high, (array - high.astype(jnp.float32)).astype(jnp.bfloat16)


def product(left, right, contract):
    def one(a, b):
        return lax.dot_general(
            a, b, (contract, ((), ())), preferred_element_type=jnp.float32
        )

    return one(left[0], right[0]) + (one(left[0], right[1]) + one(left[1], right[0]))


def prepare_kernel(
    own_centers, other_centers, own_weights, other_weights, high, low, center_sq, value_high, value_low
):
    here = own_centers.shape[0]
    outputs, lanes = own_weights.shape[0], value_high.shape[1]
    for i, (centers, weights) in enumerate(
        ((own_centers, own_weights), (other_centers, other_weights))
    ):
        place = pl.ds(i * here, here)
        turned = centers[...].T
        center_sq[:, place] = jnp.sum(turned * turned, axis=0, keepdims=True)
        high[:, place], low[:, place] = parts(turned)
        zeros = jnp.zeros((lanes - outputs, here), jnp.float32)
        padded = jnp.concatenate([weights[...], zeros], axis=0)
        value_high[place, :], value_low[place, :] = parts(padded.T)


def quarter_kernel(
    rows, centers_high, centers_low, center_sq, weights_high, weights_low, value, high, low
):
    features = rows.shape[1]
    part = rows[...]
    row_sq = jnp.sum(part * part, axis=1, keepdims=True)
    inner = product(parts(part), (centers_high[...], centers_low[...]), ((1,), (0,)))
    kernel = parts(jnp.exp((2.0 * features - row_sq - center_sq[...] + 2.0 * inner) / 128.0))
    high[...], low[...] = kernel
    value[...] = product(kernel, (weights_high[...], weights_low[...]), ((1,), (0,)))


def delta_kernel(resid_0, resid_1, resid_2, resid_3, high, low, delta, resid_high, resid_low):
    quarter = resid_0.shape[0]
    for i, resid in enumerate((resid_0, resid_1, resid_2, resid_3)):
        place = pl.ds(i * quarter, quarter)
        resid_high[place, :], resid_low[place, :] = parts(resid[...])
    found = product((high[...], low[...]), (resid_high[...], resid_low[...]), ((0,), (0,)))
    delta[...] = found.T[: delta.shape[0]]


def call(kernel, outs, *operands, scratch=()):
    return pl.pallas_call(
        kernel,
        out_shape=[jax.ShapeDtypeStruct(shape, dtype) for shape, dtype in outs],
        scratch_shapes=[pltpu.VMEM(shape, dtype) for shape, dtype in scratch],
        compiler_params=pltpu.CompilerParams(vmem_limit_bytes=VMEM_BYTES),
    )(*operands)


def per_device(batch_index, train_features, train_labels, centers, weights):
    block = batch_index.shape[0]
    features = centers.shape[1]
    outputs = weights.shape[1]
    here = centers.shape[0]
    devices = math.prod(SIZES)
    batch = block * LEVELS * 2
    scale = 1.0 / math.sqrt(here * devices)
    x, core, z = lax.axis_index("x"), lax.axis_index("core"), lax.axis_index("z")
    y_lo, y_hi = lax.axis_index("y_lo"), lax.axis_index("y_hi")
    own = block // (2 * RING * 2)
    start = (core * 2 * RING + y_lo * RING + x) * own
    index = lax.dynamic_slice_in_dim(batch_index, start, own, 0)
    rows = pick(train_features, index)
    lanes = -(-outputs // LANE) * LANE
    fill = ((0, 0), (0, lanes - outputs))
    targets = jnp.pad(pick(train_labels, index), fill)

    column, centers, own_weights = lax.optimization_barrier(
        (spread(rows, CLASSES), centers, weights)
    )
    quarter = len(CLASSES[0]) * own
    pair = 2 * here
    held = call(
        prepare_kernel,
        (
            ((features, pair), jnp.bfloat16),
            ((features, pair), jnp.bfloat16),
            ((1, pair), jnp.float32),
            ((pair, lanes), jnp.bfloat16),
            ((pair, lanes), jnp.bfloat16),
        ),
        centers,
        permute(centers, SWAP),
        own_weights.T,
        permute(own_weights, SWAP).T,
    )

    def quarter_of(part):
        return call(
            quarter_kernel,
            (
                ((quarter, lanes), jnp.float32),
                ((quarter, pair), jnp.bfloat16),
                ((quarter, pair), jnp.bfloat16),
            ),
            part,
            *held,
        )

    rows_of = quarters(column)
    done = {0: quarter_of(rows_of[0])}
    value = done[0][0]
    later = [rows_of[way] for way in WAYS]
    *later, value = lax.optimization_barrier((*later, value))
    for way, part in zip(WAYS, later):
        done[way] = quarter_of(part)
        value = value + permute(done[way][0], swap_pairs(way))
    high = jnp.concatenate([done[way][1] for way in range(4)], axis=0)
    low = jnp.concatenate([done[way][2] for way in range(4)], axis=0)
    value = scatter_sum(value, CLASSES)
    resid_of = quarters(spread(value * scale - targets, CLASSES))
    resid_list = [resid_of[way] for way in range(4)]

    def delta_of(resid, low_end, high_end):
        return call(
            delta_kernel,
            (((outputs, here), jnp.float32),),
            *resid,
            high[:, low_end:high_end],
            low[:, low_end:high_end],
            scratch=(((4 * quarter, lanes), jnp.bfloat16),) * 2,
        )[0]

    first = delta_of(resid_list, here, pair)
    received = permute(first, SWAP)
    *resid_list, first = lax.optimization_barrier((*resid_list, first))
    second = delta_of(resid_list, 0, here)
    new_weights = (weights.T - step_size / batch * (second + received)).T

    resid_all = jnp.concatenate(resid_list, axis=0)
    pieces = []
    for low in range(2):
        for column in range(RING):
            way = (x + column) % 2 + 2 * ((y_lo + low) % 2)
            slot = (column // 2 * (RING // 2) + y_hi) * LEVELS + z
            pieces.append(lax.dynamic_slice_in_dim(resid_all, way * quarter + slot * own, own, 0))
    mine = jnp.concatenate(pieces, axis=0)[:, :outputs]
    theirs = permute(mine, SWAP)
    residual = jnp.where(
        core == 0,
        jnp.concatenate([mine, theirs], axis=0),
        jnp.concatenate([theirs, mine], axis=0),
    )
    return (new_weights, residual)


def solution(mesh):
    split = Mesh(mesh.devices.reshape(SIZES), AXES)
    placed = (
        P(NARROW),
        P(NARROW, None),
        P(NARROW, None),
        P(WIDE_NARROW, None),
        P(WIDE_NARROW, None),
    )
    return jax.shard_map(
        per_device,
        mesh=split,
        in_specs=placed,
        out_specs=(P(WIDE_NARROW, None), P(NARROW, None)),
        check_vma=False,
    )
```

```python
import math

import jax
import jax.numpy as jnp
from jax import lax
from jax.experimental import pallas as pl
from jax.experimental.pallas import tpu as pltpu
from jax.sharding import Mesh
from jax.sharding import PartitionSpec as P

AXES = ("y_lo", "x", "core", "z", "y_hi")
SIZES = (2, 4, 2, 8, 2)
WIDE_NARROW = AXES
NARROW = ("z", "y_hi")
RING = 4
LEVELS = 8
LANE = 128
WAYS = (1, 2, 3)

VMEM_BYTES = 16 * 1024 * 1024

step_size = 1.0


def position(x, y, z, core):
    x, y = x % RING, y % RING
    return (((y % 2 * RING + x) * 2 + core) * LEVELS + z) * 2 + y // 2


def everywhere():
    return [
        (x, y, z, core)
        for x in range(RING)
        for y in range(RING)
        for z in range(LEVELS)
        for core in range(2)
    ]


def beside(place, core, step):
    return place + step if place // step % 2 == core else place - step


def neighbour(x, y, z, core, step, way):
    if way == 1:
        x = beside(x, core, step)
    elif way == 2:
        y = beside(y, core, step)
    elif way == 3:
        z = beside(z, core, step)
    return position(x, y, z % LEVELS, core)


def swap_pairs(step, way):
    return [(position(*device), neighbour(*device, step, way)) for device in everywhere()]


SWAP = [(position(x, y, z, core), position(x, y, z, 1 - core)) for x, y, z, core in everywhere()]
GROUPS = [
    [
        position(
            2 * (i ^ z // 2 % 2) + (low ^ z % 2), 2 * (k ^ z // 2 % 2) + (high ^ z % 2), z, core
        )
        for z in range(LEVELS)
    ]
    for low in range(2)
    for high in range(2)
    for i in range(2)
    for k in range(2)
    for core in range(2)
]


def permute(array, pairs):
    return lax.ppermute(array, AXES, pairs)


def exchange(array, groups):
    return lax.all_to_all(array, AXES, 0, 0, axis_index_groups=groups, tiled=True)


def spread(array, groups):
    count = len(groups[0])
    copies = jnp.broadcast_to(array[None], (count,) + array.shape)
    return exchange(copies.reshape((-1,) + array.shape[1:]), groups)


def scatter_sum(array, groups):
    count = len(groups[0])
    return exchange(array, groups).reshape((count, -1) + array.shape[1:]).sum(axis=0)


def gathered(own, step):
    return [own] + [permute(own, swap_pairs(step, way)) for way in WAYS]


def quarters(column):
    return gathered(jnp.concatenate(gathered(column, 2), axis=0), 1)


def folded(array):
    pieces = jnp.split(array, 4, axis=0)
    total = pieces[0]
    for way in WAYS:
        total = total + permute(pieces[way], swap_pairs(2, way))
    return total


def pick(array, index):
    return array.at[index].get(mode="promise_in_bounds")


def parts(array):
    high = array.astype(jnp.bfloat16)
    return high, (array - high.astype(jnp.float32)).astype(jnp.bfloat16)


def product(left, right, contract):
    def one(a, b):
        return lax.dot_general(
            a, b, (contract, ((), ())), preferred_element_type=jnp.float32
        )

    return one(left[0], right[0]) + (one(left[0], right[1]) + one(left[1], right[0]))


def prepare_kernel(
    own_centers, other_centers, own_weights, other_weights, high, low, center_sq, value_high, value_low
):
    here = own_centers.shape[0]
    outputs, lanes = own_weights.shape[0], value_high.shape[1]
    for i, (centers, weights) in enumerate(
        ((own_centers, own_weights), (other_centers, other_weights))
    ):
        place = pl.ds(i * here, here)
        turned = centers[...].T
        center_sq[:, place] = jnp.sum(turned * turned, axis=0, keepdims=True)
        high[:, place], low[:, place] = parts(turned)
        zeros = jnp.zeros((lanes - outputs, here), jnp.float32)
        padded = jnp.concatenate([weights[...], zeros], axis=0)
        value_high[place, :], value_low[place, :] = parts(padded.T)


def quarter_kernel(
    rows, centers_high, centers_low, center_sq, weights_high, weights_low, value, high, low
):
    features = rows.shape[1]
    part = rows[...]
    row_sq = jnp.sum(part * part, axis=1, keepdims=True)
    inner = product(parts(part), (centers_high[...], centers_low[...]), ((1,), (0,)))
    kernel = parts(jnp.exp((2.0 * features - row_sq - center_sq[...] + 2.0 * inner) / 128.0))
    high[...], low[...] = kernel
    value[...] = product(kernel, (weights_high[...], weights_low[...]), ((1,), (0,)))


def delta_kernel(resid_0, resid_1, resid_2, resid_3, high, low, delta, resid_high, resid_low):
    quarter = resid_0.shape[0]
    for i, resid in enumerate((resid_0, resid_1, resid_2, resid_3)):
        place = pl.ds(i * quarter, quarter)
        resid_high[place, :], resid_low[place, :] = parts(resid[...])
    found = product((high[...], low[...]), (resid_high[...], resid_low[...]), ((0,), (0,)))
    delta[...] = found.T[: delta.shape[0]]


def first_delta_kernel(
    source, target, resid_0, resid_1, resid_2, resid_3, high, low, delta, mine, resid_high, resid_low
):
    delta_kernel(
        resid_0, resid_1, resid_2, resid_3, high, low, delta, resid_high, resid_low
    )
    for i, resid in enumerate((resid_0, resid_1, resid_2, resid_3)):
        for j in range(2):
            for row in range(mine.shape[0] // 8):
                found = resid[pl.ds(source[i, j] + row, 1), :]
                mine[pl.ds(target[i, j] + row, 1), :] = found[:, : mine.shape[1]]


def call(kernel, outs, *operands, scratch=(), scalars=0):
    return pl.pallas_call(
        kernel,
        in_specs=[pl.BlockSpec(memory_space=pltpu.SMEM)] * scalars
        + [pl.BlockSpec(memory_space=pltpu.VMEM)] * (len(operands) - scalars),
        out_shape=[jax.ShapeDtypeStruct(shape, dtype) for shape, dtype in outs],
        scratch_shapes=[pltpu.VMEM(shape, dtype) for shape, dtype in scratch],
        compiler_params=pltpu.CompilerParams(vmem_limit_bytes=VMEM_BYTES),
    )(*operands)


def per_device(batch_index, train_features, train_labels, centers, weights):
    block = batch_index.shape[0]
    features = centers.shape[1]
    outputs = weights.shape[1]
    here = centers.shape[0]
    devices = math.prod(SIZES)
    batch = block * LEVELS * 2
    scale = 1.0 / math.sqrt(here * devices)
    x, core, z = lax.axis_index("x"), lax.axis_index("core"), lax.axis_index("z")
    y_lo, y_hi = lax.axis_index("y_lo"), lax.axis_index("y_hi")
    y = y_hi * 2 + y_lo
    own = block // (2 * RING * 2)
    start = (core * 2 * RING + y_lo * RING + x) * own
    index = lax.dynamic_slice_in_dim(batch_index, start, own, 0)
    rows = pick(train_features, index)
    lanes = -(-outputs // LANE) * LANE
    fill = ((0, 0), (0, lanes - outputs))
    targets = jnp.pad(pick(train_labels, index), fill)

    column, centers, own_weights = lax.optimization_barrier(
        (spread(rows, GROUPS), centers, weights)
    )
    column_rows = LEVELS * own
    quarter = 4 * column_rows
    pair = 2 * here
    held = call(
        prepare_kernel,
        (
            ((features, pair), jnp.bfloat16),
            ((features, pair), jnp.bfloat16),
            ((1, pair), jnp.float32),
            ((pair, lanes), jnp.bfloat16),
            ((pair, lanes), jnp.bfloat16),
        ),
        centers,
        permute(centers, SWAP),
        own_weights.T,
        permute(own_weights, SWAP).T,
    )

    def quarter_of(part):
        return call(
            quarter_kernel,
            (
                ((quarter, lanes), jnp.float32),
                ((quarter, pair), jnp.bfloat16),
                ((quarter, pair), jnp.bfloat16),
            ),
            part,
            *held,
        )

    first_rows, *later = quarters(column)
    done = [quarter_of(first_rows)]
    value = done[0][0]
    *later, value = lax.optimization_barrier((*later, value))
    for way, part in zip(WAYS, later):
        done.append(quarter_of(part))
        value = value + permute(done[way][0], swap_pairs(1, way))
    high = jnp.concatenate([part[1] for part in done], axis=0)
    low = jnp.concatenate([part[2] for part in done], axis=0)
    value = scatter_sum(folded(value), GROUPS)
    resid_list = quarters(spread(value * scale - targets, GROUPS))

    way, half = jnp.arange(4)[:, None], jnp.arange(2)[None, :]
    turn = z // 2 % 2
    next_x = jnp.where(x % 2 == core, x + 1, x - 1) % RING
    next_y = jnp.where(y % 2 == core, y + 1, y - 1) % RING
    next_z = jnp.where(z % 2 == core, z + 1, z - 1) % LEVELS
    held_turn = jnp.where(way == 3, next_z // 2 % 2, turn)
    held_x = jnp.where(way == 1, next_x, x) // 2 ^ held_turn
    held_y = jnp.where(way == 2, next_y, y) // 2 ^ held_turn
    piece = (held_x ^ half ^ turn) + 2 * (held_y ^ y_hi ^ turn)
    source = piece * column_rows + z * own
    target = ((y_lo ^ way // 2) * RING + 2 * half + ((x ^ way) % 2)) * own + 0 * source
    scratch = (((4 * quarter, lanes), jnp.bfloat16),) * 2
    delta_out = ((outputs, here), jnp.float32)
    first, mine = call(
        first_delta_kernel,
        (delta_out, ((block // 2, outputs), jnp.float32)),
        source.astype(jnp.int32),
        target.astype(jnp.int32),
        *resid_list,
        high[:, here:],
        low[:, here:],
        scratch=scratch,
        scalars=2,
    )
    received = permute(first, SWAP)
    (second,) = call(
        delta_kernel, (delta_out,), *resid_list, high[:, :here], low[:, :here], scratch=scratch
    )
    new_weights = (weights.T - step_size / batch * (second + received)).T
    theirs = permute(mine, SWAP)
    residual = jnp.where(
        core == 0,
        jnp.concatenate([mine, theirs], axis=0),
        jnp.concatenate([theirs, mine], axis=0),
    )
    return (new_weights, residual)


def solution(mesh):
    split = Mesh(mesh.devices.reshape(SIZES), AXES)
    placed = (
        P(NARROW),
        P(NARROW, None),
        P(NARROW, None),
        P(WIDE_NARROW, None),
        P(WIDE_NARROW, None),
    )
    return jax.shard_map(
        per_device,
        mesh=split,
        in_specs=placed,
        out_specs=(P(WIDE_NARROW, None), P(NARROW, None)),
        check_vma=False,
    )
```

```python
import functools
import math

import jax
import jax.numpy as jnp
from jax import lax
from jax.experimental import pallas as pl
from jax.experimental.pallas import tpu as pltpu
from jax.sharding import Mesh
from jax.sharding import PartitionSpec as P

AXES = ("y_lo", "x", "core", "z", "y_hi")
SIZES = (2, 4, 2, 8, 2)
WIDE_NARROW = AXES
NARROW = ("z", "y_hi")
RING = 4
LEVELS = 8
LANE = 128
WAYS = (1, 2, 3)

VMEM_BYTES = 16 * 1024 * 1024

step_size = 1.0


def position(x, y, z, core):
    x, y = x % RING, y % RING
    return (((y % 2 * RING + x) * 2 + core) * LEVELS + z) * 2 + y // 2


def everywhere():
    return [
        (x, y, z, core)
        for x in range(RING)
        for y in range(RING)
        for z in range(LEVELS)
        for core in range(2)
    ]


def beside(place, core):
    return place + 1 if place % 2 == core else place - 1


def neighbour(x, y, z, core, way):
    if way == 1:
        x = beside(x, core)
    elif way == 2:
        y = beside(y, core)
    elif way == 3:
        z = beside(z, core)
    return position(x, y, z % LEVELS, core)


def swap_pairs(way):
    return [(position(*device), neighbour(*device, way)) for device in everywhere()]


SWAP = [(position(x, y, z, core), position(x, y, z, 1 - core)) for x, y, z, core in everywhere()]
PLANES = [
    [
        position(2 * i + (low ^ odd), 2 * k + (high ^ odd), 2 * level + odd, core)
        for i in range(2)
        for k in range(2)
        for odd in range(2)
    ]
    for low in range(2)
    for high in range(2)
    for level in range(LEVELS // 2)
    for core in range(2)
]
COLUMNS = [
    [position(x, y, 2 * level + odd, core) for level in range(LEVELS // 2)]
    for x in range(RING)
    for y in range(RING)
    for odd in range(2)
    for core in range(2)
]


def permute(array, pairs):
    return lax.ppermute(array, AXES, pairs)


def exchange(array, groups):
    return lax.all_to_all(array, AXES, 0, 0, axis_index_groups=groups, tiled=True)


def spread(array, groups):
    count = len(groups[0])
    copies = jnp.broadcast_to(array[None], (count,) + array.shape)
    return exchange(copies.reshape((-1,) + array.shape[1:]), groups)


def scatter_sum(array, groups):
    count = len(groups[0])
    return exchange(array, groups).reshape((count, -1) + array.shape[1:]).sum(axis=0)


def quarters(own):
    return [own] + [permute(own, swap_pairs(way)) for way in WAYS]


def pick(array, index):
    return array.at[index].get(mode="promise_in_bounds")


def parts(array):
    high = array.astype(jnp.bfloat16)
    return high, (array - high.astype(jnp.float32)).astype(jnp.bfloat16)


def product(left, right, contract):
    def one(a, b):
        return lax.dot_general(
            a, b, (contract, ((), ())), preferred_element_type=jnp.float32
        )

    return one(left[0], right[0]) + (one(left[0], right[1]) + one(left[1], right[0]))


def prepare_kernel(
    own_centers, other_centers, own_weights, other_weights, high, low, center_sq, value_high, value_low
):
    here = own_centers.shape[0]
    outputs, lanes = own_weights.shape[0], value_high.shape[1]
    for i, (centers, weights) in enumerate(
        ((own_centers, own_weights), (other_centers, other_weights))
    ):
        place = pl.ds(i * here, here)
        turned = centers[...].T
        center_sq[:, place] = jnp.sum(turned * turned, axis=0, keepdims=True)
        high[:, place], low[:, place] = parts(turned)
        zeros = jnp.zeros((lanes - outputs, here), jnp.float32)
        padded = jnp.concatenate([weights[...], zeros], axis=0)
        value_high[place, :], value_low[place, :] = parts(padded.T)


def quarter_kernel(
    rows, centers_high, centers_low, center_sq, weights_high, weights_low, value, high, low
):
    features = rows.shape[1]
    part = rows[...]
    row_sq = jnp.sum(part * part, axis=1, keepdims=True)
    inner = product(parts(part), (centers_high[...], centers_low[...]), ((1,), (0,)))
    kernel = parts(jnp.exp((2.0 * features - row_sq - center_sq[...] + 2.0 * inner) / 128.0))
    high[...], low[...] = kernel
    value[...] = product(kernel, (weights_high[...], weights_low[...]), ((1,), (0,)))


def delta_kernel(
    source,
    target,
    resid_0,
    resid_1,
    resid_2,
    resid_3,
    high,
    low,
    other_delta,
    own_delta,
    mine,
    resid_high,
    resid_low,
):
    quarter = resid_0.shape[0]
    here = own_delta.shape[1]
    for i, resid in enumerate((resid_0, resid_1, resid_2, resid_3)):
        place = pl.ds(i * quarter, quarter)
        resid_high[place, :], resid_low[place, :] = parts(resid[...])
        for j in range(2):
            for row in range(mine.shape[0] // 8):
                found = resid[pl.ds(source[i, j] + row, 1), :]
                mine[pl.ds(target[i, j] + row, 1), :] = found[:, : mine.shape[1]]
    for start, delta in ((0, own_delta), (here, other_delta)):
        place = pl.ds(start, here)
        kernel = (high[:, place], low[:, place])
        found = product(kernel, (resid_high[...], resid_low[...]), ((0,), (0,)))
        delta[...] = found.T[: delta.shape[0]]


def update_kernel(factor, weights, own_delta, other_delta, out):
    out[...] = weights[...] - factor * (own_delta[...] + other_delta[...])


def update(factor, *operands):
    shape = operands[0].shape
    spec = pl.BlockSpec((shape[0] // 5, shape[1]), lambda i: (i, 0))
    return pl.pallas_call(
        functools.partial(update_kernel, factor),
        grid=(5,),
        in_specs=[spec] * len(operands),
        out_specs=spec,
        out_shape=jax.ShapeDtypeStruct(shape, jnp.float32),
        compiler_params=pltpu.CompilerParams(vmem_limit_bytes=VMEM_BYTES),
    )(*operands)


def call(kernel, outs, *operands, scratch=(), scalars=0):
    return pl.pallas_call(
        kernel,
        in_specs=[pl.BlockSpec(memory_space=pltpu.SMEM)] * scalars
        + [pl.BlockSpec(memory_space=pltpu.VMEM)] * (len(operands) - scalars),
        out_shape=[jax.ShapeDtypeStruct(shape, dtype) for shape, dtype in outs],
        scratch_shapes=[pltpu.VMEM(shape, dtype) for shape, dtype in scratch],
        compiler_params=pltpu.CompilerParams(vmem_limit_bytes=VMEM_BYTES),
    )(*operands)


def per_device(batch_index, train_features, train_labels, centers, weights):
    block = batch_index.shape[0]
    features = centers.shape[1]
    outputs = weights.shape[1]
    here = centers.shape[0]
    devices = math.prod(SIZES)
    batch = block * LEVELS * 2
    scale = 1.0 / math.sqrt(here * devices)
    x, core, z = lax.axis_index("x"), lax.axis_index("core"), lax.axis_index("z")
    y_lo, y_hi = lax.axis_index("y_lo"), lax.axis_index("y_hi")
    own = block // (2 * RING * 2)
    start = (core * 2 * RING + y_lo * RING + x) * own
    index = lax.dynamic_slice_in_dim(batch_index, start, own, 0)
    rows = pick(train_features, index)
    lanes = -(-outputs // LANE) * LANE
    fill = ((0, 0), (0, lanes - outputs))
    targets = jnp.pad(pick(train_labels, index), fill)

    column, centers, own_weights = lax.optimization_barrier(
        (spread(spread(rows, COLUMNS), PLANES), centers, weights)
    )
    levels = LEVELS // 2
    column_rows = levels * own
    quarter = len(PLANES[0]) * column_rows
    pair = 2 * here
    held = call(
        prepare_kernel,
        (
            ((features, pair), jnp.bfloat16),
            ((features, pair), jnp.bfloat16),
            ((1, pair), jnp.float32),
            ((pair, lanes), jnp.bfloat16),
            ((pair, lanes), jnp.bfloat16),
        ),
        centers,
        permute(centers, SWAP),
        own_weights.T,
        permute(own_weights, SWAP).T,
    )

    def quarter_of(part):
        return call(
            quarter_kernel,
            (
                ((quarter, lanes), jnp.float32),
                ((quarter, pair), jnp.bfloat16),
                ((quarter, pair), jnp.bfloat16),
            ),
            part,
            *held,
        )

    first_rows, *later = quarters(column)
    done = [quarter_of(first_rows)]
    value = done[0][0]
    *later, value = lax.optimization_barrier((*later, value))
    for way, part in zip(WAYS, later):
        done.append(quarter_of(part))
        value = value + permute(done[way][0], swap_pairs(way))
    high = jnp.concatenate([part[1] for part in done], axis=0)
    low = jnp.concatenate([part[2] for part in done], axis=0)
    value = scatter_sum(value, PLANES) * scale
    level = jnp.arange(levels)[:, None, None]
    value = value - jnp.where(level == z // 2, targets[None], 0.0).reshape(value.shape)
    partial_sums = spread(value, COLUMNS).reshape((levels,) + value.shape)
    resid_list = quarters(spread(partial_sums.sum(axis=0), PLANES))

    way, half = jnp.arange(4)[:, None], jnp.arange(2)[None, :]
    source = (half * 4 + y_hi * 2 + z % 2) * column_rows + z // 2 * own + 0 * way
    target = ((y_lo ^ way // 2) * RING + 2 * half + ((x ^ way) % 2)) * own
    delta_out = ((outputs, here), jnp.float32)
    first, second, mine = call(
        delta_kernel,
        (delta_out, delta_out, ((block // 2, outputs), jnp.float32)),
        source.astype(jnp.int32),
        target.astype(jnp.int32),
        *resid_list,
        high,
        low,
        scratch=(((4 * quarter, lanes), jnp.bfloat16),) * 2,
        scalars=2,
    )
    received = permute(first, SWAP)
    new_weights = update(step_size / batch, weights.T, second, received).T
    theirs = permute(mine, SWAP)
    residual = jnp.where(
        core == 0,
        jnp.concatenate([mine, theirs], axis=0),
        jnp.concatenate([theirs, mine], axis=0),
    )
    return (new_weights, residual)


def solution(mesh):
    split = Mesh(mesh.devices.reshape(SIZES), AXES)
    placed = (
        P(NARROW),
        P(NARROW, None),
        P(NARROW, None),
        P(WIDE_NARROW, None),
        P(WIDE_NARROW, None),
    )
    return jax.shard_map(
        per_device,
        mesh=split,
        in_specs=placed,
        out_specs=(P(WIDE_NARROW, None), P(NARROW, None)),
        check_vma=False,
    )
```

```python
import functools
import math

import jax
import jax.numpy as jnp
from jax import lax
from jax.experimental import pallas as pl
from jax.experimental.pallas import tpu as pltpu
from jax.sharding import Mesh
from jax.sharding import PartitionSpec as P

AXES = ("y_lo", "x", "core", "z", "y_hi")
SIZES = (2, 4, 2, 8, 2)
WIDE_NARROW = AXES
NARROW = ("z", "y_hi")
RING = 4
LEVELS = 8
LANE = 128
WAYS = (1, 2, 3)

VMEM_BYTES = 16 * 1024 * 1024

step_size = 1.0


def position(x, y, z, core):
    x, y = x % RING, y % RING
    return (((y % 2 * RING + x) * 2 + core) * LEVELS + z) * 2 + y // 2


def everywhere():
    return [
        (x, y, z, core)
        for x in range(RING)
        for y in range(RING)
        for z in range(LEVELS)
        for core in range(2)
    ]


def beside(place, core):
    return place + 1 if place % 2 == core else place - 1


def neighbour(x, y, z, core, way):
    if way == 1:
        x = beside(x, core)
    elif way == 2:
        y = beside(y, core)
    elif way == 3:
        z = beside(z, core)
    return position(x, y, z % LEVELS, core)


def swap_pairs(way):
    return [(position(*device), neighbour(*device, way)) for device in everywhere()]


SWAP = [(position(x, y, z, core), position(x, y, z, 1 - core)) for x, y, z, core in everywhere()]
PLANES = [
    [
        position(2 * i + (low ^ odd), 2 * k + (high ^ odd), 2 * level + odd, core)
        for i in range(2)
        for k in range(2)
        for odd in range(2)
    ]
    for low in range(2)
    for high in range(2)
    for level in range(LEVELS // 2)
    for core in range(2)
]
CLASSES = [
    [
        position(2 * i + (low ^ odd), 2 * k + (high ^ odd), 2 * level + odd, core)
        for i in range(2)
        for k in range(2)
        for odd in range(2)
        for level in range(LEVELS // 2)
    ]
    for low in range(2)
    for high in range(2)
    for core in range(2)
]


def along_z(step):
    return [
        (position(x, y, z, core), position(x, y, (z + step) % LEVELS, core))
        for x, y, z, core in everywhere()
    ]


def permute(array, pairs):
    return lax.ppermute(array, AXES, pairs)


def exchange(array, groups):
    return lax.all_to_all(array, AXES, 0, 0, axis_index_groups=groups, tiled=True)


def spread(array, groups):
    count = len(groups[0])
    copies = jnp.broadcast_to(array[None], (count,) + array.shape)
    return exchange(copies.reshape((-1,) + array.shape[1:]), groups)


def quarters(own):
    return [own] + [permute(own, swap_pairs(way)) for way in WAYS]


def pick(array, index):
    return array.at[index].get(mode="promise_in_bounds")


def parts(array):
    high = array.astype(jnp.bfloat16)
    return high, (array - high.astype(jnp.float32)).astype(jnp.bfloat16)


def product(left, right, contract):
    def one(a, b):
        return lax.dot_general(
            a, b, (contract, ((), ())), preferred_element_type=jnp.float32
        )

    return one(left[0], right[0]) + (one(left[0], right[1]) + one(left[1], right[0]))


def prepare_kernel(
    own_centers, other_centers, own_weights, other_weights, high, low, center_sq, value_high, value_low
):
    here = own_centers.shape[0]
    outputs, lanes = own_weights.shape[0], value_high.shape[1]
    for i, (centers, weights) in enumerate(
        ((own_centers, own_weights), (other_centers, other_weights))
    ):
        place = pl.ds(i * here, here)
        turned = centers[...].T
        center_sq[:, place] = jnp.sum(turned * turned, axis=0, keepdims=True)
        high[:, place], low[:, place] = parts(turned)
        zeros = jnp.zeros((lanes - outputs, here), jnp.float32)
        padded = jnp.concatenate([weights[...], zeros], axis=0)
        value_high[place, :], value_low[place, :] = parts(padded.T)


def quarter_kernel(
    rows, centers_high, centers_low, center_sq, weights_high, weights_low, value, high, low
):
    features = rows.shape[1]
    part = rows[...]
    row_sq = jnp.sum(part * part, axis=1, keepdims=True)
    inner = product(parts(part), (centers_high[...], centers_low[...]), ((1,), (0,)))
    kernel = parts(jnp.exp((2.0 * features - row_sq - center_sq[...] + 2.0 * inner) / 128.0))
    high[...], low[...] = kernel
    value[...] = product(kernel, (weights_high[...], weights_low[...]), ((1,), (0,)))


def targets_kernel(own, index, place, labels, out, turned):
    rows, outputs = index.shape[0], labels.shape[0]
    width = labels.shape[1]
    zeros = jnp.zeros((out.shape[1] - outputs, width), jnp.float32)
    turned[...] = jnp.concatenate([labels[...], zeros], axis=0).T
    out[...] = jnp.zeros_like(out)
    start = place[3] // 2 * own
    for row in range(rows):
        out[pl.ds(start + row, 1), :] = turned[pl.ds(index[row], 1), :]


def plane_kernel(scale, sums, targets, out):
    total = sums[0]
    for i in range(1, sums.shape[0]):
        total = total + sums[i]
    out[...] = total * scale - targets[...]


def delta_kernel(factor, place, *refs):
    resid_refs, high_refs, low_refs = refs[:4], refs[4:8], refs[8:12]
    weights, other_delta, new_weights, mine, resid_high, resid_low, high, low = refs[12:]
    quarter = resid_refs[0].shape[0]
    outputs, here = weights.shape
    own = mine.shape[0] // 8
    x, y_lo, y_hi, z = place[0], place[1], place[2], place[3]
    for way in range(4):
        resid = resid_refs[way]
        rows = pl.ds(way * quarter, quarter)
        resid_high[rows, :], resid_low[rows, :] = parts(resid[...])
        high[rows, :], low[rows, :] = high_refs[way][...], low_refs[way][...]
        for half in range(2):
            source = (half * 4 + y_hi * 2 + z % 2) * (quarter // 8) + z // 2 * own
            target = ((y_lo + way // 2) % 2 * RING + 2 * half + (x + way) % 2) * own
            for row in range(own):
                mine[pl.ds(target + row, 1), :] = resid[pl.ds(source + row, 1), :][:, :outputs]

    def delta_of(start):
        columns = pl.ds(start, here)
        found = product(
            (high[:, columns], low[:, columns]), (resid_high[...], resid_low[...]), ((0,), (0,))
        )
        return found.T[:outputs]

    other_delta[...] = delta_of(here)
    new_weights[...] = weights[...] - factor * delta_of(0)


def update_kernel(factor, weights, delta, out):
    out[...] = weights[...] - factor * delta[...]


def update(factor, *operands):
    shape = operands[0].shape
    spec = pl.BlockSpec((shape[0] // 5, shape[1]), lambda i: (i, 0))
    return pl.pallas_call(
        functools.partial(update_kernel, factor),
        grid=(5,),
        in_specs=[spec] * len(operands),
        out_specs=spec,
        out_shape=jax.ShapeDtypeStruct(shape, jnp.float32),
        compiler_params=pltpu.CompilerParams(vmem_limit_bytes=VMEM_BYTES),
    )(*operands)


def call(kernel, outs, *operands, scratch=(), scalars=0, products=0):
    return pl.pallas_call(
        kernel,
        in_specs=[pl.BlockSpec(memory_space=pltpu.SMEM)] * scalars
        + [pl.BlockSpec(memory_space=pltpu.VMEM)] * (len(operands) - scalars),
        out_shape=[jax.ShapeDtypeStruct(shape, dtype) for shape, dtype in outs],
        scratch_shapes=[pltpu.VMEM(shape, dtype) for shape, dtype in scratch],
        compiler_params=pltpu.CompilerParams(vmem_limit_bytes=VMEM_BYTES),
        cost_estimate=pl.CostEstimate(
            flops=2 * products, bytes_accessed=VMEM_BYTES // 8, transcendentals=0
        ),
    )(*operands)


def per_device(batch_index, train_features, train_labels, centers, weights):
    block = batch_index.shape[0]
    features = centers.shape[1]
    outputs = weights.shape[1]
    here = centers.shape[0]
    devices = math.prod(SIZES)
    batch = block * LEVELS * 2
    scale = 1.0 / math.sqrt(here * devices)
    x, core, z = lax.axis_index("x"), lax.axis_index("core"), lax.axis_index("z")
    y_lo, y_hi = lax.axis_index("y_lo"), lax.axis_index("y_hi")
    own = block // (2 * RING * 2)
    start = (core * 2 * RING + y_lo * RING + x) * own
    index = lax.dynamic_slice_in_dim(batch_index, start, own, 0)
    rows = pick(train_features, index)
    lanes = -(-outputs // LANE) * LANE
    place = jnp.stack([x, y_lo, y_hi, z]).astype(jnp.int32)
    rows, place = lax.optimization_barrier((rows, place))

    column, centers, own_weights, train_labels = lax.optimization_barrier(
        (spread(rows, CLASSES), centers, weights, train_labels)
    )
    column_rows = LEVELS // 2 * own
    quarter = len(CLASSES[0]) * own
    pair = 2 * here
    held = call(
        prepare_kernel,
        (
            ((features, pair), jnp.bfloat16),
            ((features, pair), jnp.bfloat16),
            ((1, pair), jnp.float32),
            ((pair, lanes), jnp.bfloat16),
            ((pair, lanes), jnp.bfloat16),
        ),
        centers,
        permute(centers, SWAP),
        own_weights.T,
        permute(own_weights, SWAP).T,
    )

    def quarter_of(part):
        return call(
            quarter_kernel,
            (
                ((quarter, lanes), jnp.float32),
                ((quarter, pair), jnp.bfloat16),
                ((quarter, pair), jnp.bfloat16),
            ),
            part,
            *held,
            products=3 * quarter * pair * (features + lanes),
        )

    first_rows, *later = quarters(column)
    done = [quarter_of(first_rows)]
    value = done[0][0]
    (targets,) = call(
        functools.partial(targets_kernel, own),
        (((column_rows, lanes), jnp.float32),),
        index,
        place,
        train_labels.T,
        scratch=(((train_labels.shape[0], lanes), jnp.float32),),
        scalars=2,
    )
    *later, value, targets = lax.optimization_barrier((*later, value, targets))
    for way, part in zip(WAYS, later):
        done.append(quarter_of(part))
        value = value + permute(done[way][0], swap_pairs(way))
    sums = exchange(value, PLANES).reshape(len(PLANES[0]), column_rows, lanes)
    (value,) = call(
        functools.partial(plane_kernel, scale), (((column_rows, lanes), jnp.float32),), sums, targets
    )
    opposite, up, down = (permute(value, along_z(step)) for step in (4, 2, -2))
    resid_list = quarters(spread((value + opposite) + (up + down), PLANES))

    factor = step_size / batch
    delta_out = ((outputs, here), jnp.float32)
    first, partly, mine = call(
        functools.partial(delta_kernel, factor),
        (delta_out, delta_out, ((block // 2, outputs), jnp.float32)),
        place,
        *resid_list,
        *(part[1] for part in done),
        *(part[2] for part in done),
        weights.T,
        scratch=(((4 * quarter, lanes), jnp.bfloat16),) * 2 + (((4 * quarter, pair), jnp.bfloat16),) * 2,
        scalars=1,
        products=3 * 4 * quarter * pair * lanes,
    )
    new_weights = update(factor, partly, permute(first, SWAP)).T
    theirs = permute(mine, SWAP)
    residual = jnp.where(
        core == 0,
        jnp.concatenate([mine, theirs], axis=0),
        jnp.concatenate([theirs, mine], axis=0),
    )
    return (new_weights, residual)


def solution(mesh):
    split = Mesh(mesh.devices.reshape(SIZES), AXES)
    placed = (
        P(NARROW),
        P(NARROW, None),
        P(NARROW, None),
        P(WIDE_NARROW, None),
        P(WIDE_NARROW, None),
    )
    return jax.shard_map(
        per_device,
        mesh=split,
        in_specs=placed,
        out_specs=(P(WIDE_NARROW, None), P(NARROW, None)),
        check_vma=False,
    )
```

```python
import functools
import math

import jax
import jax.numpy as jnp
from jax import lax
from jax.experimental import pallas as pl
from jax.experimental.pallas import tpu as pltpu
from jax.sharding import Mesh
from jax.sharding import PartitionSpec as P

AXES = ("y_lo", "x", "core", "z", "y_hi")
SIZES = (2, 4, 2, 8, 2)
WIDE_NARROW = AXES
NARROW = ("z", "y_hi")
RING = 4
LEVELS = 8
LANE = 128
WAYS = (1, 2, 3)

VMEM_BYTES = 16 * 1024 * 1024

step_size = 1.0


def position(x, y, z, core):
    x, y = x % RING, y % RING
    return (((y % 2 * RING + x) * 2 + core) * LEVELS + z) * 2 + y // 2


def everywhere():
    return [
        (x, y, z, core)
        for x in range(RING)
        for y in range(RING)
        for z in range(LEVELS)
        for core in range(2)
    ]


def beside(place, core):
    return place + 1 if place % 2 == core else place - 1


def neighbour(x, y, z, core, way):
    if way == 1:
        x = beside(x, core)
    elif way == 2:
        y = beside(y, core)
    elif way == 3:
        z = beside(z, core)
    return position(x, y, z % LEVELS, core)


def swap_pairs(way):
    return [(position(*device), neighbour(*device, way)) for device in everywhere()]


SWAP = [(position(x, y, z, core), position(x, y, z, 1 - core)) for x, y, z, core in everywhere()]
PLANES = [
    [
        position(2 * i + (low ^ odd), 2 * k + (high ^ odd), 2 * level + odd, core)
        for i in range(2)
        for k in range(2)
        for odd in range(2)
    ]
    for low in range(2)
    for high in range(2)
    for level in range(LEVELS // 2)
    for core in range(2)
]
LINES = [
    [
        position(x, first if high == 0 else RING - 1 - first, z, core)
        for high in range(2)
        for z in range(LEVELS)
    ]
    for x in range(RING)
    for first in range(2)
    for core in range(2)
]


def along_z(step):
    return [
        (position(x, y, z, core), position(x, y, (z + step) % LEVELS, core))
        for x, y, z, core in everywhere()
    ]


def permute(array, pairs):
    return lax.ppermute(array, AXES, pairs)


def exchange(array, groups):
    return lax.all_to_all(array, AXES, 0, 0, axis_index_groups=groups, tiled=True)


def spread(array, groups):
    count = len(groups[0])
    copies = jnp.broadcast_to(array[None], (count,) + array.shape)
    return exchange(copies.reshape((-1,) + array.shape[1:]), groups)


def quarters(own):
    return [own] + [permute(own, swap_pairs(way)) for way in WAYS]


def pick(array, index):
    return array.at[index].get(mode="promise_in_bounds")


def parts(array):
    high = array.astype(jnp.bfloat16)
    return high, (array - high.astype(jnp.float32)).astype(jnp.bfloat16)


def product(left, right, contract):
    def one(a, b):
        return lax.dot_general(
            a, b, (contract, ((), ())), preferred_element_type=jnp.float32
        )

    return one(left[0], right[0]) + (one(left[0], right[1]) + one(left[1], right[0]))


def prepare_kernel(
    own_centers, other_centers, own_weights, other_weights, high, low, center_sq, value_high, value_low
):
    here = own_centers.shape[0]
    outputs, lanes = own_weights.shape[0], value_high.shape[1]
    for i, (centers, weights) in enumerate(
        ((own_centers, own_weights), (other_centers, other_weights))
    ):
        place = pl.ds(i * here, here)
        turned = centers[...].T
        center_sq[:, place] = jnp.sum(turned * turned, axis=0, keepdims=True)
        high[:, place], low[:, place] = parts(turned)
        zeros = jnp.zeros((lanes - outputs, here), jnp.float32)
        padded = jnp.concatenate([weights[...], zeros], axis=0)
        value_high[place, :], value_low[place, :] = parts(padded.T)


def quarter_kernel(
    rows, centers_high, centers_low, center_sq, weights_high, weights_low, value, high, low
):
    features = rows.shape[1]
    part = rows[...]
    row_sq = jnp.sum(part * part, axis=1, keepdims=True)
    inner = product(parts(part), (centers_high[...], centers_low[...]), ((1,), (0,)))
    kernel = parts(jnp.exp((2.0 * features - row_sq - center_sq[...] + 2.0 * inner) / 128.0))
    high[...], low[...] = kernel
    value[...] = product(kernel, (weights_high[...], weights_low[...]), ((1,), (0,)))


def order_kernel(own, found, out):
    levels = LEVELS // 2
    for i in range(2):
        for k in range(2):
            for odd in range(2):
                for level in range(levels):
                    source = (((k * levels + level) * 2 + odd) * 2 + i) * own
                    target = (((i * 2 + k) * 2 + odd) * levels + level) * own
                    out[target : target + own, :] = found[source : source + own, :]


def targets_kernel(own, index, place, labels, out, turned):
    rows, outputs = index.shape[0], labels.shape[0]
    width = labels.shape[1]
    zeros = jnp.zeros((out.shape[1] - outputs, width), jnp.float32)
    turned[...] = jnp.concatenate([labels[...], zeros], axis=0).T
    out[...] = jnp.zeros_like(out)
    start = place[3] // 2 * own
    for row in range(rows):
        out[pl.ds(start + row, 1), :] = turned[pl.ds(index[row], 1), :]


def plane_kernel(scale, sums, targets, out):
    total = sums[0]
    for i in range(1, sums.shape[0]):
        total = total + sums[i]
    out[...] = total * scale - targets[...]


def delta_kernel(start, place, *refs):
    resid_refs, high_refs, low_refs = refs[:4], refs[4:8], refs[8:12]
    delta, *mine, resid_high, resid_low, high, low = refs[12:]
    quarter = resid_refs[0].shape[0]
    outputs, here = delta.shape
    columns = pl.ds(start, here)
    x, y_lo, y_hi, z = place[0], place[1], place[2], place[3]
    for way in range(4):
        resid = resid_refs[way]
        rows = pl.ds(way * quarter, quarter)
        resid_high[rows, :], resid_low[rows, :] = parts(resid[...])
        high[rows, :], low[rows, :] = high_refs[way][:, columns], low_refs[way][:, columns]
        for out in mine:
            own = out.shape[0] // 8
            for half in range(2):
                source = (half * 4 + y_hi * 2 + z % 2) * (quarter // 8) + z // 2 * own
                target = ((y_lo + way // 2) % 2 * RING + 2 * half + (x + way) % 2) * own
                for row in range(own):
                    out[pl.ds(target + row, 1), :] = resid[pl.ds(source + row, 1), :][:, :outputs]
    found = product((high[...], low[...]), (resid_high[...], resid_low[...]), ((0,), (0,)))
    delta[...] = found.T[:outputs]


def update_kernel(factor, place, weights, own_delta, other_delta, mine, theirs, out, residual):
    rows = mine.shape[0]
    core = place[4]
    residual[pl.ds(pl.multiple_of(core * rows, 8), rows), :] = mine[...]
    residual[pl.ds(pl.multiple_of((1 - core) * rows, 8), rows), :] = theirs[...]
    out[...] = weights[...] - factor * (own_delta[...] + other_delta[...])


def call(kernel, outs, *operands, scratch=(), scalars=0, products=0):
    return pl.pallas_call(
        kernel,
        in_specs=[pl.BlockSpec(memory_space=pltpu.SMEM)] * scalars
        + [pl.BlockSpec(memory_space=pltpu.VMEM)] * (len(operands) - scalars),
        out_shape=[jax.ShapeDtypeStruct(shape, dtype) for shape, dtype in outs],
        scratch_shapes=[pltpu.VMEM(shape, dtype) for shape, dtype in scratch],
        compiler_params=pltpu.CompilerParams(vmem_limit_bytes=VMEM_BYTES),
        cost_estimate=pl.CostEstimate(
            flops=2 * products, bytes_accessed=VMEM_BYTES // 8, transcendentals=0
        ),
    )(*operands)


def per_device(batch_index, train_features, train_labels, centers, weights):
    block = batch_index.shape[0]
    features = centers.shape[1]
    outputs = weights.shape[1]
    here = centers.shape[0]
    devices = math.prod(SIZES)
    batch = block * LEVELS * 2
    scale = 1.0 / math.sqrt(here * devices)
    x, core, z = lax.axis_index("x"), lax.axis_index("core"), lax.axis_index("z")
    y_lo, y_hi = lax.axis_index("y_lo"), lax.axis_index("y_hi")
    own = block // (2 * RING * 2)
    start = (core * 2 * RING + y_lo * RING + x) * own
    index = lax.dynamic_slice_in_dim(batch_index, start, own, 0)
    lanes = -(-outputs // LANE) * LANE
    half_block = block // 2
    order = jnp.arange(half_block)
    high, odd, far, row = order // (4 * own), order // (2 * own) % 2, order // own % 2, order % own
    turn = odd ^ z % 2
    wanted = ((y_lo ^ y_hi ^ high ^ turn) * RING + 2 * far + (x % 2 ^ turn)) * own + row
    match = (core * half_block + wanted)[:, None] == jnp.arange(block)[None, :]
    wanted_index = jnp.sum(jnp.where(match, batch_index[None, :], 0), axis=1)
    rows = pick(train_features, wanted_index)
    place = jnp.stack([x, y_lo, y_hi, z, core]).astype(jnp.int32)
    rows, place = lax.optimization_barrier((rows, place))
    sent = jnp.broadcast_to(
        rows.reshape(2, 1, 2, 2 * own, features), (2, LEVELS // 2, 2, 2 * own, features)
    )
    found = exchange(sent.reshape(-1, features), LINES)
    found, centers, own_weights, train_labels = lax.optimization_barrier(
        (found, centers, weights, train_labels)
    )
    (column,) = call(
        functools.partial(order_kernel, own), ((found.shape, jnp.float32),), found
    )
    column_rows = LEVELS // 2 * own
    quarter = found.shape[0]
    pair = 2 * here
    held = call(
        prepare_kernel,
        (
            ((features, pair), jnp.bfloat16),
            ((features, pair), jnp.bfloat16),
            ((1, pair), jnp.float32),
            ((pair, lanes), jnp.bfloat16),
            ((pair, lanes), jnp.bfloat16),
        ),
        centers,
        permute(centers, SWAP),
        own_weights.T,
        permute(own_weights, SWAP).T,
    )

    def quarter_of(part):
        return call(
            quarter_kernel,
            (
                ((quarter, lanes), jnp.float32),
                ((quarter, pair), jnp.bfloat16),
                ((quarter, pair), jnp.bfloat16),
            ),
            part,
            *held,
            products=3 * quarter * pair * (features + lanes),
        )

    first_rows, *later = quarters(column)
    done = [quarter_of(first_rows)]
    value = done[0][0]
    (targets,) = call(
        functools.partial(targets_kernel, own),
        (((column_rows, lanes), jnp.float32),),
        index,
        place,
        train_labels.T,
        scratch=(((train_labels.shape[0], lanes), jnp.float32),),
        scalars=2,
    )
    sums = []
    for way, part in zip(WAYS, later):
        part, value, targets = lax.optimization_barrier((part, value, targets))
        done.append(quarter_of(part))
        sums.append(permute(done[way][0], swap_pairs(way)))
    for found in sums:
        value = value + found
    sums = exchange(value, PLANES).reshape(len(PLANES[0]), column_rows, lanes)
    (value,) = call(
        functools.partial(plane_kernel, scale), (((column_rows, lanes), jnp.float32),), sums, targets
    )
    opposite, up, down = (permute(value, along_z(step)) for step in (4, 2, -2))
    resid_list = quarters(spread((value + opposite) + (up + down), PLANES))

    def delta_of(start, *outs):
        return call(
            functools.partial(delta_kernel, start),
            (((outputs, here), jnp.float32), *outs),
            place,
            *resid_list,
            *(part[1] for part in done),
            *(part[2] for part in done),
            scratch=(((4 * quarter, lanes), jnp.bfloat16),) * 2
            + (((4 * quarter, here), jnp.bfloat16),) * 2,
            scalars=1,
            products=3 * 4 * quarter * here * lanes,
        )

    first, mine = delta_of(here, ((half_block, outputs), jnp.float32))
    received, theirs = permute(first, SWAP), permute(mine, SWAP)
    *resid_list, first = lax.optimization_barrier((*resid_list, first))
    (second,) = delta_of(0)
    new_weights, residual = call(
        functools.partial(update_kernel, step_size / batch),
        (((outputs, here), jnp.float32), ((block, outputs), jnp.float32)),
        place,
        weights.T,
        second,
        received,
        mine,
        theirs,
        scalars=1,
    )
    return (new_weights.T, residual)


def solution(mesh):
    split = Mesh(mesh.devices.reshape(SIZES), AXES)
    placed = (
        P(NARROW),
        P(NARROW, None),
        P(NARROW, None),
        P(WIDE_NARROW, None),
        P(WIDE_NARROW, None),
    )
    return jax.shard_map(
        per_device,
        mesh=split,
        in_specs=placed,
        out_specs=(P(WIDE_NARROW, None), P(NARROW, None)),
        check_vma=False,
    )
```

```python
import functools
import math

import jax
import jax.numpy as jnp
from jax import lax
from jax.experimental import pallas as pl
from jax.experimental.pallas import tpu as pltpu
from jax.sharding import Mesh
from jax.sharding import PartitionSpec as P

AXES = ("y_lo", "x", "core", "z", "y_hi")
SIZES = (2, 4, 2, 8, 2)
WIDE_NARROW = AXES
NARROW = ("z", "y_hi")
RING = 4
LEVELS = 8
LANE = 128
WAYS = (1, 2, 3)

VMEM_BYTES = 16 * 1024 * 1024

step_size = 1.0


def position(x, y, z, core):
    x, y = x % RING, y % RING
    return (((y % 2 * RING + x) * 2 + core) * LEVELS + z) * 2 + y // 2


def everywhere():
    return [
        (x, y, z, core)
        for x in range(RING)
        for y in range(RING)
        for z in range(LEVELS)
        for core in range(2)
    ]


def beside(place, core):
    return place + 1 if place % 2 == core else place - 1


def neighbour(x, y, z, core, way):
    if way == 1:
        x = beside(x, core)
    elif way == 2:
        y = beside(y, core)
    elif way == 3:
        z = beside(z, core)
    return position(x, y, z % LEVELS, core)


def swap_pairs(way):
    return [(position(*device), neighbour(*device, way)) for device in everywhere()]


SWAP = [(position(x, y, z, core), position(x, y, z, 1 - core)) for x, y, z, core in everywhere()]
PLANES = [
    [
        position(2 * i + (low ^ odd), 2 * k + (high ^ odd), 2 * level + odd, core)
        for i in range(2)
        for k in range(2)
        for odd in range(2)
    ]
    for low in range(2)
    for high in range(2)
    for level in range(LEVELS // 2)
    for core in range(2)
]
LINES = [
    [
        position(x, first if high == 0 else RING - 1 - first, z, core)
        for high in range(2)
        for z in range(LEVELS)
    ]
    for x in range(RING)
    for first in range(2)
    for core in range(2)
]


def along_z(step):
    return [
        (position(x, y, z, core), position(x, y, (z + step) % LEVELS, core))
        for x, y, z, core in everywhere()
    ]


def permute(array, pairs):
    return lax.ppermute(array, AXES, pairs)


def exchange(array, groups):
    return lax.all_to_all(array, AXES, 0, 0, axis_index_groups=groups, tiled=True)


def spread(array, groups):
    count = len(groups[0])
    copies = jnp.broadcast_to(array[None], (count,) + array.shape)
    return exchange(copies.reshape((-1,) + array.shape[1:]), groups)


def quarters(own):
    return [own] + [permute(own, swap_pairs(way)) for way in WAYS]


def pick(array, index):
    return array.at[index].get(mode="promise_in_bounds")


def parts(array):
    high = array.astype(jnp.bfloat16)
    return high, (array - high.astype(jnp.float32)).astype(jnp.bfloat16)


def product(left, right, contract):
    def one(a, b):
        return lax.dot_general(
            a, b, (contract, ((), ())), preferred_element_type=jnp.float32
        )

    return one(left[0], right[0]) + (one(left[0], right[1]) + one(left[1], right[0]))


def prepare_kernel(
    own,
    index,
    place,
    own_centers,
    other_centers,
    own_weights,
    other_weights,
    labels,
    high,
    low,
    center_sq,
    value_high,
    value_low,
    targets,
    turned_labels,
):
    here = own_centers.shape[0]
    outputs, lanes = own_weights.shape[0], value_high.shape[1]

    def padded(array):
        zeros = jnp.zeros((lanes - outputs, array.shape[1]), jnp.float32)
        return jnp.concatenate([array, zeros], axis=0).T

    for i, (centers, weights) in enumerate(
        ((own_centers, own_weights), (other_centers, other_weights))
    ):
        columns = pl.ds(i * here, here)
        turned = centers[...].T
        center_sq[:, columns] = jnp.sum(turned * turned, axis=0, keepdims=True)
        high[:, columns], low[:, columns] = parts(turned)
        value_high[columns, :], value_low[columns, :] = parts(padded(weights[...]))
    turned_labels[...] = padded(labels[...])
    targets[...] = jnp.zeros_like(targets)
    start = place[3] // 2 * own
    for row in range(own):
        targets[pl.ds(start + row, 1), :] = turned_labels[pl.ds(index[row], 1), :]


def quarter_kernel(
    rows, centers_high, centers_low, center_sq, weights_high, weights_low, value, high, low
):
    features = rows.shape[1]
    part = rows[...]
    row_sq = jnp.sum(part * part, axis=1, keepdims=True)
    inner = product(parts(part), (centers_high[...], centers_low[...]), ((1,), (0,)))
    kernel = parts(jnp.exp((2.0 * features - row_sq - center_sq[...] + 2.0 * inner) / 128.0))
    high[...], low[...] = kernel
    value[...] = product(kernel, (weights_high[...], weights_low[...]), ((1,), (0,)))


def order_kernel(own, found, out):
    levels = LEVELS // 2
    for i in range(2):
        for k in range(2):
            for odd in range(2):
                for level in range(levels):
                    source = (((k * levels + level) * 2 + odd) * 2 + i) * own
                    target = (((i * 2 + k) * 2 + odd) * levels + level) * own
                    out[target : target + own, :] = found[source : source + own, :]


def plane_kernel(scale, sums, targets, out):
    total = sums[0]
    for i in range(1, sums.shape[0]):
        total = total + sums[i]
    out[...] = total * scale - targets[...]


def delta_kernel(start, place, *refs):
    resid_refs, high_refs, low_refs = refs[:4], refs[4:8], refs[8:12]
    delta, *mine, resid_high, resid_low, high, low = refs[12:]
    quarter = resid_refs[0].shape[0]
    outputs, here = delta.shape
    columns = pl.ds(start, here)
    x, y_lo, y_hi, z = place[0], place[1], place[2], place[3]
    for way in range(4):
        resid = resid_refs[way]
        rows = pl.ds(way * quarter, quarter)
        resid_high[rows, :], resid_low[rows, :] = parts(resid[...])
        high[rows, :], low[rows, :] = high_refs[way][:, columns], low_refs[way][:, columns]
        for out in mine:
            own = out.shape[0] // 8
            for half in range(2):
                source = (half * 4 + y_hi * 2 + z % 2) * (quarter // 8) + z // 2 * own
                target = ((y_lo + way // 2) % 2 * RING + 2 * half + (x + way) % 2) * own
                for row in range(own):
                    out[pl.ds(target + row, 1), :] = resid[pl.ds(source + row, 1), :][:, :outputs]
    found = product((high[...], low[...]), (resid_high[...], resid_low[...]), ((0,), (0,)))
    delta[...] = found.T[:outputs]


def update_kernel(factor, place, weights, own_delta, other_delta, mine, theirs, out, residual):
    rows = mine.shape[0]
    core = place[4]
    residual[pl.ds(pl.multiple_of(core * rows, 8), rows), :] = mine[...]
    residual[pl.ds(pl.multiple_of((1 - core) * rows, 8), rows), :] = theirs[...]
    out[...] = weights[...] - factor * (own_delta[...] + other_delta[...])


def call(kernel, outs, *operands, scratch=(), scalars=0, products=0):
    return pl.pallas_call(
        kernel,
        in_specs=[pl.BlockSpec(memory_space=pltpu.SMEM)] * scalars
        + [pl.BlockSpec(memory_space=pltpu.VMEM)] * (len(operands) - scalars),
        out_shape=[jax.ShapeDtypeStruct(shape, dtype) for shape, dtype in outs],
        scratch_shapes=[pltpu.VMEM(shape, dtype) for shape, dtype in scratch],
        compiler_params=pltpu.CompilerParams(vmem_limit_bytes=VMEM_BYTES),
        cost_estimate=pl.CostEstimate(
            flops=2 * products, bytes_accessed=VMEM_BYTES // 8, transcendentals=0
        ),
    )(*operands)


def per_device(batch_index, train_features, train_labels, centers, weights):
    block = batch_index.shape[0]
    features = centers.shape[1]
    outputs = weights.shape[1]
    here = centers.shape[0]
    devices = math.prod(SIZES)
    batch = block * LEVELS * 2
    scale = 1.0 / math.sqrt(here * devices)
    x, core, z = lax.axis_index("x"), lax.axis_index("core"), lax.axis_index("z")
    y_lo, y_hi = lax.axis_index("y_lo"), lax.axis_index("y_hi")
    own = block // (2 * RING * 2)
    start = (core * 2 * RING + y_lo * RING + x) * own
    index = lax.dynamic_slice_in_dim(batch_index, start, own, 0)
    lanes = -(-outputs // LANE) * LANE
    half_block = block // 2
    order = jnp.arange(half_block)
    high, odd, far, row = order // (4 * own), order // (2 * own) % 2, order // own % 2, order % own
    turn = odd ^ z % 2
    wanted = ((y_lo ^ y_hi ^ high ^ turn) * RING + 2 * far + (x % 2 ^ turn)) * own + row
    match = (core * half_block + wanted)[:, None] == jnp.arange(block)[None, :]
    wanted_index = jnp.sum(jnp.where(match, batch_index[None, :], 0), axis=1)
    rows = pick(train_features, wanted_index)
    place = jnp.stack([x, y_lo, y_hi, z, core]).astype(jnp.int32)
    rows, place, index = lax.optimization_barrier((rows, place, index))
    sent = jnp.broadcast_to(
        rows.reshape(2, 1, 2, 2 * own, features), (2, LEVELS // 2, 2, 2 * own, features)
    )
    found = exchange(sent.reshape(-1, features), LINES)
    found, centers, own_weights, train_labels = lax.optimization_barrier(
        (found, centers, weights, train_labels)
    )
    (column,) = call(
        functools.partial(order_kernel, own), ((found.shape, jnp.float32),), found
    )
    column_rows = LEVELS // 2 * own
    quarter = found.shape[0]
    pair = 2 * here
    *held, targets = call(
        functools.partial(prepare_kernel, own),
        (
            ((features, pair), jnp.bfloat16),
            ((features, pair), jnp.bfloat16),
            ((1, pair), jnp.float32),
            ((pair, lanes), jnp.bfloat16),
            ((pair, lanes), jnp.bfloat16),
            ((column_rows, lanes), jnp.float32),
        ),
        index,
        place,
        centers,
        permute(centers, SWAP),
        own_weights.T,
        permute(own_weights, SWAP).T,
        train_labels.T,
        scratch=(((train_labels.shape[0], lanes), jnp.float32),),
        scalars=2,
    )

    def quarter_of(part):
        return call(
            quarter_kernel,
            (
                ((quarter, lanes), jnp.float32),
                ((quarter, pair), jnp.bfloat16),
                ((quarter, pair), jnp.bfloat16),
            ),
            part,
            *held,
            products=3 * quarter * pair * (features + lanes),
        )

    first_rows, *later = quarters(column)
    done = [quarter_of(first_rows)]
    value = done[0][0]
    sums = []
    for way, part in zip(WAYS, later):
        part, value = lax.optimization_barrier((part, value))
        done.append(quarter_of(part))
        sums.append(permute(done[way][0], swap_pairs(way)))
    for found in sums:
        value = value + found
    sums = exchange(value, PLANES).reshape(len(PLANES[0]), column_rows, lanes)
    (value,) = call(
        functools.partial(plane_kernel, scale), (((column_rows, lanes), jnp.float32),), sums, targets
    )
    opposite, up, down = (permute(value, along_z(step)) for step in (4, 2, -2))
    resid_list = quarters(spread((value + opposite) + (up + down), PLANES))

    def delta_of(start, *outs):
        return call(
            functools.partial(delta_kernel, start),
            (((outputs, here), jnp.float32), *outs),
            place,
            *resid_list,
            *(part[1] for part in done),
            *(part[2] for part in done),
            scratch=(((4 * quarter, lanes), jnp.bfloat16),) * 2
            + (((4 * quarter, here), jnp.bfloat16),) * 2,
            scalars=1,
            products=3 * 4 * quarter * here * lanes,
        )

    first, mine = delta_of(here, ((half_block, outputs), jnp.float32))
    received, theirs = permute(first, SWAP), permute(mine, SWAP)
    *resid_list, first = lax.optimization_barrier((*resid_list, first))
    (second,) = delta_of(0)
    new_weights, residual = call(
        functools.partial(update_kernel, step_size / batch),
        (((outputs, here), jnp.float32), ((block, outputs), jnp.float32)),
        place,
        weights.T,
        second,
        received,
        mine,
        theirs,
        scalars=1,
    )
    return (new_weights.T, residual)


def solution(mesh):
    split = Mesh(mesh.devices.reshape(SIZES), AXES)
    placed = (
        P(NARROW),
        P(NARROW, None),
        P(NARROW, None),
        P(WIDE_NARROW, None),
        P(WIDE_NARROW, None),
    )
    return jax.shard_map(
        per_device,
        mesh=split,
        in_specs=placed,
        out_specs=(P(WIDE_NARROW, None), P(NARROW, None)),
        check_vma=False,
    )
```

```python
import functools
import math

import jax
import jax.numpy as jnp
from jax import lax
from jax.experimental import pallas as pl
from jax.experimental.pallas import tpu as pltpu
from jax.sharding import Mesh
from jax.sharding import PartitionSpec as P

AXES = ("y_lo", "x", "core", "z", "y_hi")
SIZES = (2, 4, 2, 8, 2)
WIDE_NARROW = AXES
NARROW = ("z", "y_hi")
RING = 4
LEVELS = 8
LANE = 128
WAYS = (1, 2, 3)

VMEM_BYTES = 16 * 1024 * 1024

step_size = 1.0


def position(x, y, z, core):
    x, y = x % RING, y % RING
    return (((y % 2 * RING + x) * 2 + core) * LEVELS + z) * 2 + y // 2


def everywhere():
    return [
        (x, y, z, core)
        for x in range(RING)
        for y in range(RING)
        for z in range(LEVELS)
        for core in range(2)
    ]


def beside(place, core):
    return place + 1 if place % 2 == core else place - 1


def neighbour(x, y, z, core, way):
    if way == 1:
        x = beside(x, core)
    elif way == 2:
        y = beside(y, core)
    elif way == 3:
        z = beside(z, core)
    return position(x, y, z % LEVELS, core)


def swap_pairs(way):
    return [(position(*device), neighbour(*device, way)) for device in everywhere()]


SWAP = [(position(x, y, z, core), position(x, y, z, 1 - core)) for x, y, z, core in everywhere()]
PLANES = [
    [
        position(2 * i + (low ^ odd), 2 * k + (high ^ odd), 2 * level + odd, core)
        for i in range(2)
        for k in range(2)
        for odd in range(2)
    ]
    for low in range(2)
    for high in range(2)
    for level in range(LEVELS // 2)
    for core in range(2)
]
LINES = [
    [
        position(x, first if high == 0 else RING - 1 - first, z, core)
        for high in range(2)
        for z in range(LEVELS)
    ]
    for x in range(RING)
    for first in range(2)
    for core in range(2)
]


def along_z(step):
    return [
        (position(x, y, z, core), position(x, y, (z + step) % LEVELS, core))
        for x, y, z, core in everywhere()
    ]


def permute(array, pairs):
    return lax.ppermute(array, AXES, pairs)


def exchange(array, groups):
    return lax.all_to_all(array, AXES, 0, 0, axis_index_groups=groups, tiled=True)


def spread(array, groups):
    count = len(groups[0])
    copies = jnp.broadcast_to(array[None], (count,) + array.shape)
    return exchange(copies.reshape((-1,) + array.shape[1:]), groups)


def quarters(own):
    return [own] + [permute(own, swap_pairs(way)) for way in WAYS]


def pick(array, index):
    return array.at[index].get(mode="promise_in_bounds")


def parts(array):
    high = array.astype(jnp.bfloat16)
    return high, (array - high.astype(jnp.float32)).astype(jnp.bfloat16)


def product(left, right, contract):
    def one(a, b):
        return lax.dot_general(
            a, b, (contract, ((), ())), preferred_element_type=jnp.float32
        )

    return one(left[0], right[0]) + (one(left[0], right[1]) + one(left[1], right[0]))


def prepare_kernel(
    own,
    index,
    place,
    own_centers,
    other_centers,
    own_weights,
    other_weights,
    labels,
    high,
    low,
    center_sq,
    value_high,
    value_low,
    targets,
    turned_labels,
):
    here = own_centers.shape[0]
    outputs, lanes = own_weights.shape[0], value_high.shape[1]

    def padded(array):
        zeros = jnp.zeros((lanes - outputs, array.shape[1]), jnp.float32)
        return jnp.concatenate([array, zeros], axis=0).T

    for i, (centers, weights) in enumerate(
        ((own_centers, own_weights), (other_centers, other_weights))
    ):
        columns = pl.ds(i * here, here)
        turned = centers[...].T
        center_sq[:, columns] = jnp.sum(turned * turned, axis=0, keepdims=True)
        high[:, columns], low[:, columns] = parts(turned)
        value_high[columns, :], value_low[columns, :] = parts(padded(weights[...]))
    turned_labels[...] = padded(labels[...])
    targets[...] = jnp.zeros_like(targets)
    start = place[3] // 2 * own
    for row in range(own):
        targets[pl.ds(start + row, 1), :] = turned_labels[pl.ds(index[row], 1), :]


def quarters_kernel(count, *refs):
    rows, refs = refs[:count], refs[count:]
    centers_high, centers_low, center_sq, weights_high, weights_low = refs[:5]
    values, highs, lows = (refs[5 + i * count : 5 + (i + 1) * count] for i in range(3))
    quarter, features = rows[0].shape
    part = jnp.concatenate([ref[...] for ref in rows], axis=0)
    row_sq = jnp.sum(part * part, axis=1, keepdims=True)
    inner = product(parts(part), (centers_high[...], centers_low[...]), ((1,), (0,)))
    kernel = parts(jnp.exp((2.0 * features - row_sq - center_sq[...] + 2.0 * inner) / 128.0))
    value = product(kernel, (weights_high[...], weights_low[...]), ((1,), (0,)))
    for i in range(count):
        place = slice(i * quarter, (i + 1) * quarter)
        values[i][...] = value[place]
        highs[i][...] = kernel[0][place]
        lows[i][...] = kernel[1][place]


def order_kernel(own, found, out):
    levels = LEVELS // 2
    for i in range(2):
        for k in range(2):
            for odd in range(2):
                for level in range(levels):
                    source = (((k * levels + level) * 2 + odd) * 2 + i) * own
                    target = (((i * 2 + k) * 2 + odd) * levels + level) * own
                    out[target : target + own, :] = found[source : source + own, :]


def plane_kernel(scale, sums, targets, out):
    total = sums[0]
    for i in range(1, sums.shape[0]):
        total = total + sums[i]
    out[...] = total * scale - targets[...]


def delta_kernel(start, place, *refs):
    resid_refs, high_refs, low_refs = refs[:4], refs[4:8], refs[8:12]
    delta, *mine, resid_high, resid_low, high, low = refs[12:]
    quarter = resid_refs[0].shape[0]
    outputs, here = delta.shape
    columns = pl.ds(start, here)
    x, y_lo, y_hi, z = place[0], place[1], place[2], place[3]
    for way in range(4):
        resid = resid_refs[way]
        rows = pl.ds(way * quarter, quarter)
        resid_high[rows, :], resid_low[rows, :] = parts(resid[...])
        high[rows, :], low[rows, :] = high_refs[way][:, columns], low_refs[way][:, columns]
        for out in mine:
            own = out.shape[0] // 8
            for half in range(2):
                source = (half * 4 + y_hi * 2 + z % 2) * (quarter // 8) + z // 2 * own
                target = ((y_lo + way // 2) % 2 * RING + 2 * half + (x + way) % 2) * own
                for row in range(own):
                    out[pl.ds(target + row, 1), :] = resid[pl.ds(source + row, 1), :][:, :outputs]
    found = product((high[...], low[...]), (resid_high[...], resid_low[...]), ((0,), (0,)))
    delta[...] = found.T[:outputs]


def update_kernel(factor, place, weights, own_delta, other_delta, mine, theirs, out, residual):
    rows = mine.shape[0]
    core = place[4]
    residual[pl.ds(pl.multiple_of(core * rows, 8), rows), :] = mine[...]
    residual[pl.ds(pl.multiple_of((1 - core) * rows, 8), rows), :] = theirs[...]
    out[...] = weights[...] - factor * (own_delta[...] + other_delta[...])


def call(kernel, outs, *operands, scratch=(), scalars=0, products=0):
    return pl.pallas_call(
        kernel,
        in_specs=[pl.BlockSpec(memory_space=pltpu.SMEM)] * scalars
        + [pl.BlockSpec(memory_space=pltpu.VMEM)] * (len(operands) - scalars),
        out_shape=[jax.ShapeDtypeStruct(shape, dtype) for shape, dtype in outs],
        scratch_shapes=[pltpu.VMEM(shape, dtype) for shape, dtype in scratch],
        compiler_params=pltpu.CompilerParams(vmem_limit_bytes=VMEM_BYTES),
        cost_estimate=pl.CostEstimate(
            flops=2 * products, bytes_accessed=VMEM_BYTES // 8, transcendentals=0
        ),
    )(*operands)


def per_device(batch_index, train_features, train_labels, centers, weights):
    block = batch_index.shape[0]
    features = centers.shape[1]
    outputs = weights.shape[1]
    here = centers.shape[0]
    devices = math.prod(SIZES)
    batch = block * LEVELS * 2
    scale = 1.0 / math.sqrt(here * devices)
    x, core, z = lax.axis_index("x"), lax.axis_index("core"), lax.axis_index("z")
    y_lo, y_hi = lax.axis_index("y_lo"), lax.axis_index("y_hi")
    own = block // (2 * RING * 2)
    start = (core * 2 * RING + y_lo * RING + x) * own
    index = lax.dynamic_slice_in_dim(batch_index, start, own, 0)
    lanes = -(-outputs // LANE) * LANE
    half_block = block // 2
    order = jnp.arange(half_block)
    high, odd, far, row = order // (4 * own), order // (2 * own) % 2, order // own % 2, order % own
    turn = odd ^ z % 2
    wanted = ((y_lo ^ y_hi ^ high ^ turn) * RING + 2 * far + (x % 2 ^ turn)) * own + row
    match = (core * half_block + wanted)[:, None] == jnp.arange(block)[None, :]
    wanted_index = jnp.sum(jnp.where(match, batch_index[None, :], 0), axis=1)
    rows = pick(train_features, wanted_index)
    place = jnp.stack([x, y_lo, y_hi, z, core]).astype(jnp.int32)
    rows, place, index, own_centers, own_weights = lax.optimization_barrier(
        (rows, place, index, centers, weights)
    )
    other_centers, other_weights = permute(own_centers, SWAP), permute(own_weights, SWAP)
    sent = jnp.broadcast_to(
        rows.reshape(2, 1, 2, 2 * own, features), (2, LEVELS // 2, 2, 2 * own, features)
    )
    found = exchange(sent.reshape(-1, features), LINES)
    found, own_centers, own_weights, other_centers, other_weights, train_labels = (
        lax.optimization_barrier(
            (found, own_centers, own_weights, other_centers, other_weights, train_labels)
        )
    )
    (column,) = call(
        functools.partial(order_kernel, own), ((found.shape, jnp.float32),), found
    )
    column_rows = LEVELS // 2 * own
    quarter = found.shape[0]
    pair = 2 * here
    *held, targets = call(
        functools.partial(prepare_kernel, own),
        (
            ((features, pair), jnp.bfloat16),
            ((features, pair), jnp.bfloat16),
            ((1, pair), jnp.float32),
            ((pair, lanes), jnp.bfloat16),
            ((pair, lanes), jnp.bfloat16),
            ((column_rows, lanes), jnp.float32),
        ),
        index,
        place,
        own_centers,
        other_centers,
        own_weights.T,
        other_weights.T,
        train_labels.T,
        scratch=(((train_labels.shape[0], lanes), jnp.float32),),
        scalars=2,
    )

    def quarters_of(*rows):
        count = len(rows)
        found = call(
            functools.partial(quarters_kernel, count),
            (((quarter, lanes), jnp.float32),) * count
            + (((quarter, pair), jnp.bfloat16),) * 2 * count,
            *rows,
            *held,
            products=3 * count * quarter * pair * (features + lanes),
        )
        return list(zip(found[:count], found[count : 2 * count], found[2 * count :]))

    first_rows, *later = quarters(column)
    done = quarters_of(first_rows)
    value = done[0][0]
    *later, value = lax.optimization_barrier((*later, value))
    done += quarters_of(*later)
    sums = [permute(done[way][0], swap_pairs(way)) for way in WAYS]
    for found in sums:
        value = value + found
    sums = exchange(value, PLANES).reshape(len(PLANES[0]), column_rows, lanes)
    (value,) = call(
        functools.partial(plane_kernel, scale), (((column_rows, lanes), jnp.float32),), sums, targets
    )
    opposite, up, down = (permute(value, along_z(step)) for step in (4, 2, -2))
    resid_list = quarters(spread((value + opposite) + (up + down), PLANES))

    def delta_of(start, *outs):
        return call(
            functools.partial(delta_kernel, start),
            (((outputs, here), jnp.float32), *outs),
            place,
            *resid_list,
            *(part[1] for part in done),
            *(part[2] for part in done),
            scratch=(((4 * quarter, lanes), jnp.bfloat16),) * 2
            + (((4 * quarter, here), jnp.bfloat16),) * 2,
            scalars=1,
            products=3 * 4 * quarter * here * lanes,
        )

    first, mine = delta_of(here, ((half_block, outputs), jnp.float32))
    received, theirs = permute(first, SWAP), permute(mine, SWAP)
    *resid_list, first = lax.optimization_barrier((*resid_list, first))
    (second,) = delta_of(0)
    new_weights, residual = call(
        functools.partial(update_kernel, step_size / batch),
        (((outputs, here), jnp.float32), ((block, outputs), jnp.float32)),
        place,
        weights.T,
        second,
        received,
        mine,
        theirs,
        scalars=1,
    )
    return (new_weights.T, residual)


def solution(mesh):
    split = Mesh(mesh.devices.reshape(SIZES), AXES)
    placed = (
        P(NARROW),
        P(NARROW, None),
        P(NARROW, None),
        P(WIDE_NARROW, None),
        P(WIDE_NARROW, None),
    )
    return jax.shard_map(
        per_device,
        mesh=split,
        in_specs=placed,
        out_specs=(P(WIDE_NARROW, None), P(NARROW, None)),
        check_vma=False,
    )
```

```python
import functools
import math

import jax
import jax.numpy as jnp
from jax import lax
from jax.experimental import pallas as pl
from jax.experimental.pallas import tpu as pltpu
from jax.sharding import Mesh
from jax.sharding import PartitionSpec as P

AXES = ("y_lo", "x", "core", "z", "y_hi")
SIZES = (2, 4, 2, 8, 2)
WIDE_NARROW = AXES
NARROW = ("z", "y_hi")
RING = 4
LEVELS = 8
LANE = 128
WAYS = (1, 2, 3)

VMEM_BYTES = 16 * 1024 * 1024

step_size = 1.0


def position(x, y, z, core):
    x, y = x % RING, y % RING
    return (((y % 2 * RING + x) * 2 + core) * LEVELS + z) * 2 + y // 2


def everywhere():
    return [
        (x, y, z, core)
        for x in range(RING)
        for y in range(RING)
        for z in range(LEVELS)
        for core in range(2)
    ]


def beside(place, core):
    return place + 1 if place % 2 == core else place - 1


def neighbour(x, y, z, core, way):
    if way == 1:
        x = beside(x, core)
    elif way == 2:
        y = beside(y, core)
    elif way == 3:
        z = beside(z, core)
    return position(x, y, z % LEVELS, core)


def swap_pairs(way):
    return [(position(*device), neighbour(*device, way)) for device in everywhere()]


SWAP = [(position(x, y, z, core), position(x, y, z, 1 - core)) for x, y, z, core in everywhere()]
PLANES = [
    [
        position(2 * i + (low ^ odd), 2 * k + (high ^ odd), 2 * level + odd, core)
        for i in range(2)
        for k in range(2)
        for odd in range(2)
    ]
    for low in range(2)
    for high in range(2)
    for level in range(LEVELS // 2)
    for core in range(2)
]
LINES = [
    [
        position(x, first if high == 0 else RING - 1 - first, z, core)
        for high in range(2)
        for z in range(LEVELS)
    ]
    for x in range(RING)
    for first in range(2)
    for core in range(2)
]


def along_z(step):
    return [
        (position(x, y, z, core), position(x, y, (z + step) % LEVELS, core))
        for x, y, z, core in everywhere()
    ]


def permute(array, pairs):
    return lax.ppermute(array, AXES, pairs)


def exchange(array, groups):
    return lax.all_to_all(array, AXES, 0, 0, axis_index_groups=groups, tiled=True)


def spread(array, groups):
    count = len(groups[0])
    copies = jnp.broadcast_to(array[None], (count,) + array.shape)
    return exchange(copies.reshape((-1,) + array.shape[1:]), groups)


def quarters(own):
    return [own] + [permute(own, swap_pairs(way)) for way in WAYS]


def pick(array, index):
    return array.at[index].get(mode="promise_in_bounds")


def parts(array):
    high = array.astype(jnp.bfloat16)
    return high, (array - high.astype(jnp.float32)).astype(jnp.bfloat16)


def product(left, right, contract):
    def one(a, b):
        return lax.dot_general(
            a, b, (contract, ((), ())), preferred_element_type=jnp.float32
        )

    return one(left[0], right[0]) + (one(left[0], right[1]) + one(left[1], right[0]))


def prepare_kernel(
    own,
    index,
    place,
    own_centers,
    other_centers,
    own_weights,
    other_weights,
    labels,
    high,
    low,
    center_sq,
    value_high,
    value_low,
    targets,
    turned_labels,
):
    here = own_centers.shape[0]
    outputs, lanes = own_weights.shape[0], value_high.shape[1]

    def padded(array):
        zeros = jnp.zeros((lanes - outputs, array.shape[1]), jnp.float32)
        return jnp.concatenate([array, zeros], axis=0).T

    for i, (centers, weights) in enumerate(
        ((own_centers, own_weights), (other_centers, other_weights))
    ):
        columns = pl.ds(i * here, here)
        turned = centers[...].T
        center_sq[:, columns] = jnp.sum(turned * turned, axis=0, keepdims=True)
        high[:, columns], low[:, columns] = parts(turned)
        value_high[columns, :], value_low[columns, :] = parts(padded(weights[...]))
    turned_labels[...] = padded(labels[...])
    targets[...] = jnp.zeros_like(targets)
    start = place[3] // 2 * own
    for row in range(own):
        targets[pl.ds(start + row, 1), :] = turned_labels[pl.ds(index[row], 1), :]


def quarter_kernel(
    rows, centers_high, centers_low, center_sq, weights_high, weights_low, value, high, low
):
    features = rows.shape[1]
    part = rows[...]
    row_sq = jnp.sum(part * part, axis=1, keepdims=True)
    inner = product(parts(part), (centers_high[...], centers_low[...]), ((1,), (0,)))
    kernel = parts(jnp.exp((2.0 * features - row_sq - center_sq[...] + 2.0 * inner) / 128.0))
    high[...], low[...] = kernel
    value[...] = product(kernel, (weights_high[...], weights_low[...]), ((1,), (0,)))


def order_kernel(own, found, out):
    levels = LEVELS // 2
    for i in range(2):
        for k in range(2):
            for odd in range(2):
                for level in range(levels):
                    source = (((k * levels + level) * 2 + odd) * 2 + i) * own
                    target = (((i * 2 + k) * 2 + odd) * levels + level) * own
                    out[target : target + own, :] = found[source : source + own, :]


def plane_kernel(scale, sums, targets, out):
    total = sums[0]
    for i in range(1, sums.shape[0]):
        total = total + sums[i]
    out[...] = total * scale - targets[...]


def delta_kernel(start, place, *refs):
    resid_refs, high_refs, low_refs = refs[:4], refs[4:8], refs[8:12]
    delta, *mine, resid_high, resid_low, high, low = refs[12:]
    quarter = resid_refs[0].shape[0]
    outputs, here = delta.shape
    columns = pl.ds(start, here)
    x, y_lo, y_hi, z = place[0], place[1], place[2], place[3]
    for way in range(4):
        resid = resid_refs[way]
        rows = pl.ds(way * quarter, quarter)
        resid_high[rows, :], resid_low[rows, :] = parts(resid[...])
        high[rows, :], low[rows, :] = high_refs[way][:, columns], low_refs[way][:, columns]
        for out in mine:
            own = out.shape[0] // 8
            for half in range(2):
                source = (half * 4 + y_hi * 2 + z % 2) * (quarter // 8) + z // 2 * own
                target = ((y_lo + way // 2) % 2 * RING + 2 * half + (x + way) % 2) * own
                for row in range(own):
                    out[pl.ds(target + row, 1), :] = resid[pl.ds(source + row, 1), :][:, :outputs]
    found = product((high[...], low[...]), (resid_high[...], resid_low[...]), ((0,), (0,)))
    delta[...] = found.T[:outputs]


def update_kernel(factor, place, weights, own_delta, other_delta, mine, theirs, out, residual):
    rows = mine.shape[0]
    core = place[4]
    residual[pl.ds(pl.multiple_of(core * rows, 8), rows), :] = mine[...]
    residual[pl.ds(pl.multiple_of((1 - core) * rows, 8), rows), :] = theirs[...]
    out[...] = weights[...] - factor * (own_delta[...] + other_delta[...])


def call(kernel, outs, *operands, scratch=(), scalars=0, products=0):
    return pl.pallas_call(
        kernel,
        in_specs=[pl.BlockSpec(memory_space=pltpu.SMEM)] * scalars
        + [pl.BlockSpec(memory_space=pltpu.VMEM)] * (len(operands) - scalars),
        out_shape=[jax.ShapeDtypeStruct(shape, dtype) for shape, dtype in outs],
        scratch_shapes=[pltpu.VMEM(shape, dtype) for shape, dtype in scratch],
        compiler_params=pltpu.CompilerParams(vmem_limit_bytes=VMEM_BYTES),
        cost_estimate=pl.CostEstimate(
            flops=2 * products, bytes_accessed=VMEM_BYTES // 8, transcendentals=0
        ),
    )(*operands)


def per_device(batch_index, train_features, train_labels, centers, weights):
    block = batch_index.shape[0]
    features = centers.shape[1]
    outputs = weights.shape[1]
    here = centers.shape[0]
    devices = math.prod(SIZES)
    batch = block * LEVELS * 2
    scale = 1.0 / math.sqrt(here * devices)
    x, core, z = lax.axis_index("x"), lax.axis_index("core"), lax.axis_index("z")
    y_lo, y_hi = lax.axis_index("y_lo"), lax.axis_index("y_hi")
    own = block // (2 * RING * 2)
    start = (core * 2 * RING + y_lo * RING + x) * own
    index = lax.dynamic_slice_in_dim(batch_index, start, own, 0)
    lanes = -(-outputs // LANE) * LANE
    half_block = block // 2
    order = jnp.arange(half_block)
    high, odd, far, row = order // (4 * own), order // (2 * own) % 2, order // own % 2, order % own
    turn = odd ^ z % 2
    wanted = ((y_lo ^ y_hi ^ high ^ turn) * RING + 2 * far + (x % 2 ^ turn)) * own + row
    match = (core * half_block + wanted)[:, None] == jnp.arange(block)[None, :]
    wanted_index = jnp.sum(jnp.where(match, batch_index[None, :], 0), axis=1)
    rows = pick(train_features, wanted_index)
    place = jnp.stack([x, y_lo, y_hi, z, core]).astype(jnp.int32)
    rows, place, index, own_centers, own_weights = lax.optimization_barrier(
        (rows, place, index, centers, weights)
    )
    other_centers, other_weights = permute(own_centers, SWAP), permute(own_weights, SWAP)
    sent = jnp.broadcast_to(
        rows.reshape(2, 1, 2, 2 * own, features), (2, LEVELS // 2, 2, 2 * own, features)
    )
    found = exchange(sent.reshape(-1, features), LINES)
    found, own_centers, own_weights, other_centers, other_weights, train_labels = (
        lax.optimization_barrier(
            (found, own_centers, own_weights, other_centers, other_weights, train_labels)
        )
    )
    (column,) = call(
        functools.partial(order_kernel, own), ((found.shape, jnp.float32),), found
    )
    column_rows = LEVELS // 2 * own
    quarter = found.shape[0]
    pair = 2 * here
    *held, targets = call(
        functools.partial(prepare_kernel, own),
        (
            ((features, pair), jnp.bfloat16),
            ((features, pair), jnp.bfloat16),
            ((1, pair), jnp.float32),
            ((pair, lanes), jnp.bfloat16),
            ((pair, lanes), jnp.bfloat16),
            ((column_rows, lanes), jnp.float32),
        ),
        index,
        place,
        own_centers,
        other_centers,
        own_weights.T,
        other_weights.T,
        train_labels.T,
        scratch=(((train_labels.shape[0], lanes), jnp.float32),),
        scalars=2,
    )

    def quarter_of(part):
        return call(
            quarter_kernel,
            (
                ((quarter, lanes), jnp.float32),
                ((quarter, pair), jnp.bfloat16),
                ((quarter, pair), jnp.bfloat16),
            ),
            part,
            *held,
            products=3 * quarter * pair * (features + lanes),
        )

    first_rows, *later = quarters(column)
    done = [quarter_of(first_rows)]
    value = done[0][0]
    sums = []
    for way, part in zip(WAYS, later):
        part, value = lax.optimization_barrier((part, value))
        done.append(quarter_of(part))
        sums.append(permute(done[way][0], swap_pairs(way)))
    for found in sums:
        value = value + found
    sums = exchange(value, PLANES).reshape(len(PLANES[0]), column_rows, lanes)
    (value,) = call(
        functools.partial(plane_kernel, scale), (((column_rows, lanes), jnp.float32),), sums, targets
    )
    opposite, up, down = (permute(value, along_z(step)) for step in (4, 2, -2))
    resid_list = quarters(spread((value + opposite) + (up + down), PLANES))

    def delta_of(start, *outs):
        return call(
            functools.partial(delta_kernel, start),
            (((outputs, here), jnp.float32), *outs),
            place,
            *resid_list,
            *(part[1] for part in done),
            *(part[2] for part in done),
            scratch=(((4 * quarter, lanes), jnp.bfloat16),) * 2
            + (((4 * quarter, here), jnp.bfloat16),) * 2,
            scalars=1,
            products=3 * 4 * quarter * here * lanes,
        )

    first, mine = delta_of(here, ((half_block, outputs), jnp.float32))
    received, theirs = permute(first, SWAP), permute(mine, SWAP)
    *resid_list, first = lax.optimization_barrier((*resid_list, first))
    (second,) = delta_of(0)
    new_weights, residual = call(
        functools.partial(update_kernel, step_size / batch),
        (((outputs, here), jnp.float32), ((block, outputs), jnp.float32)),
        place,
        weights.T,
        second,
        received,
        mine,
        theirs,
        scalars=1,
    )
    return (new_weights.T, residual)


def solution(mesh):
    split = Mesh(mesh.devices.reshape(SIZES), AXES)
    placed = (
        P(NARROW),
        P(NARROW, None),
        P(NARROW, None),
        P(WIDE_NARROW, None),
        P(WIDE_NARROW, None),
    )
    return jax.shard_map(
        per_device,
        mesh=split,
        in_specs=placed,
        out_specs=(P(WIDE_NARROW, None), P(NARROW, None)),
        check_vma=False,
    )
```

```python
import functools
import math

import jax
import jax.numpy as jnp
from jax import lax
from jax.experimental import pallas as pl
from jax.experimental.pallas import tpu as pltpu
from jax.sharding import Mesh
from jax.sharding import PartitionSpec as P

AXES = ("y_lo", "x", "core", "z", "y_hi")
SIZES = (2, 4, 2, 8, 2)
WIDE_NARROW = AXES
NARROW = ("z", "y_hi")
RING = 4
LEVELS = 8
LANE = 128
WAYS = (1, 2, 3)

VMEM_BYTES = 16 * 1024 * 1024

step_size = 1.0


def position(x, y, z, core):
    x, y = x % RING, y % RING
    return (((y % 2 * RING + x) * 2 + core) * LEVELS + z) * 2 + y // 2


def everywhere():
    return [
        (x, y, z, core)
        for x in range(RING)
        for y in range(RING)
        for z in range(LEVELS)
        for core in range(2)
    ]


def beside(place, core):
    return place + 1 if place % 2 == core else place - 1


def neighbour(x, y, z, core, way):
    if way == 1:
        x = beside(x, core)
    elif way == 2:
        y = beside(y, core)
    elif way == 3:
        z = beside(z, core)
    return position(x, y, z % LEVELS, core)


def swap_pairs(way):
    return [(position(*device), neighbour(*device, way)) for device in everywhere()]


SWAP = [(position(x, y, z, core), position(x, y, z, 1 - core)) for x, y, z, core in everywhere()]
PLANES = [
    [
        position(2 * i + (low ^ odd), 2 * k + (high ^ odd), 2 * level + odd, core)
        for i in range(2)
        for k in range(2)
        for odd in range(2)
    ]
    for low in range(2)
    for high in range(2)
    for level in range(LEVELS // 2)
    for core in range(2)
]
LINES = [
    [
        position(x, first if high == 0 else RING - 1 - first, z, core)
        for high in range(2)
        for z in range(LEVELS)
    ]
    for x in range(RING)
    for first in range(2)
    for core in range(2)
]


def along_z(step):
    return [
        (position(x, y, z, core), position(x, y, (z + step) % LEVELS, core))
        for x, y, z, core in everywhere()
    ]


def permute(array, pairs):
    return lax.ppermute(array, AXES, pairs)


def exchange(array, groups):
    return lax.all_to_all(array, AXES, 0, 0, axis_index_groups=groups, tiled=True)


def spread(array, groups):
    count = len(groups[0])
    copies = jnp.broadcast_to(array[None], (count,) + array.shape)
    return exchange(copies.reshape((-1,) + array.shape[1:]), groups)


def quarters(own):
    return [own] + [permute(own, swap_pairs(way)) for way in WAYS]


def pick(array, index):
    return array.at[index].get(mode="promise_in_bounds")


def parts(array):
    high = array.astype(jnp.bfloat16)
    return high, (array - high.astype(jnp.float32)).astype(jnp.bfloat16)


def product(left, right, contract):
    def one(a, b):
        return lax.dot_general(
            a, b, (contract, ((), ())), preferred_element_type=jnp.float32
        )

    return one(left[0], right[0]) + (one(left[0], right[1]) + one(left[1], right[0]))


def prepare_kernel(
    own,
    index,
    place,
    own_centers,
    other_centers,
    own_weights,
    other_weights,
    labels,
    high,
    low,
    center_sq,
    value_high,
    value_low,
    targets,
    turned_labels,
):
    here = own_centers.shape[0]
    outputs, lanes = own_weights.shape[0], value_high.shape[1]

    def padded(array):
        zeros = jnp.zeros((lanes - outputs, array.shape[1]), jnp.float32)
        return jnp.concatenate([array, zeros], axis=0).T

    for i, (centers, weights) in enumerate(
        ((own_centers, own_weights), (other_centers, other_weights))
    ):
        columns = pl.ds(i * here, here)
        turned = centers[...].T
        center_sq[:, columns] = jnp.sum(turned * turned, axis=0, keepdims=True)
        high[:, columns], low[:, columns] = parts(turned)
        value_high[columns, :], value_low[columns, :] = parts(padded(weights[...]))
    turned_labels[...] = padded(labels[...])
    targets[...] = jnp.zeros_like(targets)
    start = place[3] // 2 * own
    for row in range(own):
        targets[pl.ds(start + row, 1), :] = turned_labels[pl.ds(index[row], 1), :]


def quarter_kernel(
    rows, centers_high, centers_low, center_sq, weights_high, weights_low, value, high, low
):
    features = rows.shape[1]
    part = rows[...]
    row_sq = jnp.sum(part * part, axis=1, keepdims=True)
    inner = stacked_product(parts(part), (centers_high[...], centers_low[...]))
    kernel = parts(jnp.exp((2.0 * features - row_sq - center_sq[...] + 2.0 * inner) / 128.0))
    high[...], low[...] = kernel
    value[...] = stacked_product(kernel, (weights_high[...], weights_low[...]))


def stacked_product(left, right):
    def one(a, b):
        return jnp.dot(a, b, preferred_element_type=jnp.float32)

    rows = left[0].shape[0]
    both = one(jnp.concatenate(left, axis=0), right[0])
    return both[:rows] + (one(left[0], right[1]) + both[rows:])


def order_kernel(own, found, out):
    levels = LEVELS // 2
    for i in range(2):
        for k in range(2):
            for odd in range(2):
                for level in range(levels):
                    source = (((k * levels + level) * 2 + odd) * 2 + i) * own
                    target = (((i * 2 + k) * 2 + odd) * levels + level) * own
                    out[target : target + own, :] = found[source : source + own, :]


def plane_kernel(scale, sums, targets, out):
    total = sums[0]
    for i in range(1, sums.shape[0]):
        total = total + sums[i]
    out[...] = total * scale - targets[...]


def delta_kernel(start, place, *refs):
    resid_refs, high_refs, low_refs = refs[:4], refs[4:8], refs[8:12]
    delta, *mine, resid_high, resid_low, high, low = refs[12:]
    quarter = resid_refs[0].shape[0]
    outputs, here = delta.shape
    columns = pl.ds(start, here)
    x, y_lo, y_hi, z = place[0], place[1], place[2], place[3]
    for way in range(4):
        resid = resid_refs[way]
        rows = pl.ds(way * quarter, quarter)
        resid_high[rows, :], resid_low[rows, :] = parts(resid[...])
        high[rows, :], low[rows, :] = high_refs[way][:, columns], low_refs[way][:, columns]
        for out in mine:
            own = out.shape[0] // 8
            for half in range(2):
                source = (half * 4 + y_hi * 2 + z % 2) * (quarter // 8) + z // 2 * own
                target = ((y_lo + way // 2) % 2 * RING + 2 * half + (x + way) % 2) * own
                for row in range(own):
                    out[pl.ds(target + row, 1), :] = resid[pl.ds(source + row, 1), :][:, :outputs]
    found = product((high[...], low[...]), (resid_high[...], resid_low[...]), ((0,), (0,)))
    delta[...] = found.T[:outputs]


def update_kernel(factor, place, weights, own_delta, other_delta, mine, theirs, out, residual):
    rows = mine.shape[0]
    core = place[4]
    residual[pl.ds(pl.multiple_of(core * rows, 8), rows), :] = mine[...]
    residual[pl.ds(pl.multiple_of((1 - core) * rows, 8), rows), :] = theirs[...]
    out[...] = weights[...] - factor * (own_delta[...] + other_delta[...])


def call(kernel, outs, *operands, scratch=(), scalars=0, products=0):
    return pl.pallas_call(
        kernel,
        in_specs=[pl.BlockSpec(memory_space=pltpu.SMEM)] * scalars
        + [pl.BlockSpec(memory_space=pltpu.VMEM)] * (len(operands) - scalars),
        out_shape=[jax.ShapeDtypeStruct(shape, dtype) for shape, dtype in outs],
        scratch_shapes=[pltpu.VMEM(shape, dtype) for shape, dtype in scratch],
        compiler_params=pltpu.CompilerParams(vmem_limit_bytes=VMEM_BYTES),
        cost_estimate=pl.CostEstimate(
            flops=2 * products, bytes_accessed=VMEM_BYTES // 8, transcendentals=0
        ),
    )(*operands)


def per_device(batch_index, train_features, train_labels, centers, weights):
    block = batch_index.shape[0]
    features = centers.shape[1]
    outputs = weights.shape[1]
    here = centers.shape[0]
    devices = math.prod(SIZES)
    batch = block * LEVELS * 2
    scale = 1.0 / math.sqrt(here * devices)
    x, core, z = lax.axis_index("x"), lax.axis_index("core"), lax.axis_index("z")
    y_lo, y_hi = lax.axis_index("y_lo"), lax.axis_index("y_hi")
    own = block // (2 * RING * 2)
    start = (core * 2 * RING + y_lo * RING + x) * own
    index = lax.dynamic_slice_in_dim(batch_index, start, own, 0)
    lanes = -(-outputs // LANE) * LANE
    half_block = block // 2
    order = jnp.arange(half_block)
    high, odd, far, row = order // (4 * own), order // (2 * own) % 2, order // own % 2, order % own
    turn = odd ^ z % 2
    wanted = ((y_lo ^ y_hi ^ high ^ turn) * RING + 2 * far + (x % 2 ^ turn)) * own + row
    match = (core * half_block + wanted)[:, None] == jnp.arange(block)[None, :]
    wanted_index = jnp.sum(jnp.where(match, batch_index[None, :], 0), axis=1)
    rows = pick(train_features, wanted_index)
    place = jnp.stack([x, y_lo, y_hi, z, core]).astype(jnp.int32)
    rows, place, index, own_centers, own_weights = lax.optimization_barrier(
        (rows, place, index, centers, weights)
    )
    other_centers, other_weights = permute(own_centers, SWAP), permute(own_weights, SWAP)
    sent = jnp.broadcast_to(
        rows.reshape(2, 1, 2, 2 * own, features), (2, LEVELS // 2, 2, 2 * own, features)
    )
    found = exchange(sent.reshape(-1, features), LINES)
    found, own_centers, own_weights, other_centers, other_weights, train_labels = (
        lax.optimization_barrier(
            (found, own_centers, own_weights, other_centers, other_weights, train_labels)
        )
    )
    (column,) = call(
        functools.partial(order_kernel, own), ((found.shape, jnp.float32),), found
    )
    column_rows = LEVELS // 2 * own
    quarter = found.shape[0]
    pair = 2 * here
    *held, targets = call(
        functools.partial(prepare_kernel, own),
        (
            ((features, pair), jnp.bfloat16),
            ((features, pair), jnp.bfloat16),
            ((1, pair), jnp.float32),
            ((pair, lanes), jnp.bfloat16),
            ((pair, lanes), jnp.bfloat16),
            ((column_rows, lanes), jnp.float32),
        ),
        index,
        place,
        own_centers,
        other_centers,
        own_weights.T,
        other_weights.T,
        train_labels.T,
        scratch=(((train_labels.shape[0], lanes), jnp.float32),),
        scalars=2,
    )

    def quarter_of(part):
        return call(
            quarter_kernel,
            (
                ((quarter, lanes), jnp.float32),
                ((quarter, pair), jnp.bfloat16),
                ((quarter, pair), jnp.bfloat16),
            ),
            part,
            *held,
            products=3 * quarter * pair * (features + lanes),
        )

    first_rows, *later = quarters(column)
    done = [quarter_of(first_rows)]
    value = done[0][0]
    sums = []
    for way, part in zip(WAYS, later):
        part, value = lax.optimization_barrier((part, value))
        done.append(quarter_of(part))
        sums.append(permute(done[way][0], swap_pairs(way)))
    for found in sums:
        value = value + found
    sums = exchange(value, PLANES).reshape(len(PLANES[0]), column_rows, lanes)
    (value,) = call(
        functools.partial(plane_kernel, scale), (((column_rows, lanes), jnp.float32),), sums, targets
    )
    opposite, up, down = (permute(value, along_z(step)) for step in (4, 2, -2))
    resid_list = quarters(spread((value + opposite) + (up + down), PLANES))

    def delta_of(start, *outs):
        return call(
            functools.partial(delta_kernel, start),
            (((outputs, here), jnp.float32), *outs),
            place,
            *resid_list,
            *(part[1] for part in done),
            *(part[2] for part in done),
            scratch=(((4 * quarter, lanes), jnp.bfloat16),) * 2
            + (((4 * quarter, here), jnp.bfloat16),) * 2,
            scalars=1,
            products=3 * 4 * quarter * here * lanes,
        )

    first, mine = delta_of(here, ((half_block, outputs), jnp.float32))
    received, theirs = permute(first, SWAP), permute(mine, SWAP)
    *resid_list, first = lax.optimization_barrier((*resid_list, first))
    (second,) = delta_of(0)
    new_weights, residual = call(
        functools.partial(update_kernel, step_size / batch),
        (((outputs, here), jnp.float32), ((block, outputs), jnp.float32)),
        place,
        weights.T,
        second,
        received,
        mine,
        theirs,
        scalars=1,
    )
    return (new_weights.T, residual)


def solution(mesh):
    split = Mesh(mesh.devices.reshape(SIZES), AXES)
    placed = (
        P(NARROW),
        P(NARROW, None),
        P(NARROW, None),
        P(WIDE_NARROW, None),
        P(WIDE_NARROW, None),
    )
    return jax.shard_map(
        per_device,
        mesh=split,
        in_specs=placed,
        out_specs=(P(WIDE_NARROW, None), P(NARROW, None)),
        check_vma=False,
    )
```

```python
import functools
import math

import jax
import jax.numpy as jnp
from jax import lax
from jax.experimental import pallas as pl
from jax.experimental.pallas import tpu as pltpu
from jax.sharding import Mesh
from jax.sharding import PartitionSpec as P

AXES = ("y_lo", "x", "core", "z", "y_hi")
SIZES = (2, 4, 2, 8, 2)
WIDE_NARROW = AXES
NARROW = ("z", "y_hi")
RING = 4
LEVELS = 8
LANE = 128
WAYS = (1, 2, 3)

VMEM_BYTES = 16 * 1024 * 1024

step_size = 1.0


def position(x, y, z, core):
    x, y = x % RING, y % RING
    return (((y % 2 * RING + x) * 2 + core) * LEVELS + z) * 2 + y // 2


def everywhere():
    return [
        (x, y, z, core)
        for x in range(RING)
        for y in range(RING)
        for z in range(LEVELS)
        for core in range(2)
    ]


def beside(place, core):
    return place + 1 if place % 2 == core else place - 1


def neighbour(x, y, z, core, way):
    if way == 1:
        x = beside(x, core)
    elif way == 2:
        y = beside(y, core)
    elif way == 3:
        z = beside(z, core)
    return position(x, y, z % LEVELS, core)


def swap_pairs(way):
    return [(position(*device), neighbour(*device, way)) for device in everywhere()]


SWAP = [(position(x, y, z, core), position(x, y, z, 1 - core)) for x, y, z, core in everywhere()]
PLANES = [
    [
        position(2 * i + (low ^ odd), 2 * k + (high ^ odd), 2 * level + odd, core)
        for i in range(2)
        for k in range(2)
        for odd in range(2)
    ]
    for low in range(2)
    for high in range(2)
    for level in range(LEVELS // 2)
    for core in range(2)
]
LINES = [
    [
        position(x, first if high == 0 else RING - 1 - first, z, core)
        for high in range(2)
        for z in range(LEVELS)
    ]
    for x in range(RING)
    for first in range(2)
    for core in range(2)
]


def along_z(step):
    return [
        (position(x, y, z, core), position(x, y, (z + step) % LEVELS, core))
        for x, y, z, core in everywhere()
    ]


def permute(array, pairs):
    return lax.ppermute(array, AXES, pairs)


def exchange(array, groups):
    return lax.all_to_all(array, AXES, 0, 0, axis_index_groups=groups, tiled=True)


def spread(array, groups):
    count = len(groups[0])
    copies = jnp.broadcast_to(array[None], (count,) + array.shape)
    return exchange(copies.reshape((-1,) + array.shape[1:]), groups)


def quarters(own):
    return [own] + [permute(own, swap_pairs(way)) for way in WAYS]


def pick(array, index):
    return array.at[index].get(mode="promise_in_bounds")


def parts(array):
    high = array.astype(jnp.bfloat16)
    return high, (array - high.astype(jnp.float32)).astype(jnp.bfloat16)


def product(left, right, contract):
    def one(a, b):
        return lax.dot_general(
            a, b, (contract, ((), ())), preferred_element_type=jnp.float32
        )

    return one(left[0], right[0]) + (one(left[0], right[1]) + one(left[1], right[0]))


def prepare_kernel(
    own,
    index,
    place,
    own_centers,
    other_centers,
    own_weights,
    other_weights,
    labels,
    high,
    low,
    center_sq,
    value_high,
    value_low,
    targets,
    turned_labels,
):
    here = own_centers.shape[0]
    outputs, lanes = own_weights.shape[0], value_high.shape[1]

    def padded(array):
        zeros = jnp.zeros((lanes - outputs, array.shape[1]), jnp.float32)
        return jnp.concatenate([array, zeros], axis=0).T

    for i, (centers, weights) in enumerate(
        ((own_centers, own_weights), (other_centers, other_weights))
    ):
        columns = pl.ds(i * here, here)
        turned = centers[...].T
        center_sq[:, columns] = jnp.sum(turned * turned, axis=0, keepdims=True)
        high[:, columns], low[:, columns] = parts(turned)
        value_high[columns, :], value_low[columns, :] = parts(padded(weights[...]))
    turned_labels[...] = padded(labels[...])
    targets[...] = jnp.zeros_like(targets)
    start = place[3] // 2 * own
    for row in range(own):
        targets[pl.ds(start + row, 1), :] = turned_labels[pl.ds(index[row], 1), :]


def quarter_kernel(
    rows, centers_high, centers_low, center_sq, weights_high, weights_low, value, high, low
):
    features = rows.shape[1]
    part = rows[...]
    row_sq = jnp.sum(part * part, axis=1, keepdims=True)
    inner = stacked_product(parts(part), (centers_high[...], centers_low[...]))
    kernel = parts(jnp.exp((2.0 * features - row_sq - center_sq[...] + 2.0 * inner) / 128.0))
    high[...], low[...] = kernel
    value[...] = stacked_product(kernel, (weights_high[...], weights_low[...]))


def stacked_product(left, right):
    def one(a, b):
        return jnp.dot(a, b, preferred_element_type=jnp.float32)

    rows = left[0].shape[0]
    both = one(jnp.concatenate(left, axis=0), right[0])
    return both[:rows] + (one(left[0], right[1]) + both[rows:])


def order_kernel(own, found, out):
    levels = LEVELS // 2
    for i in range(2):
        for k in range(2):
            for odd in range(2):
                for level in range(levels):
                    source = (((k * levels + level) * 2 + odd) * 2 + i) * own
                    target = (((i * 2 + k) * 2 + odd) * levels + level) * own
                    out[target : target + own, :] = found[source : source + own, :]


def plane_kernel(scale, sums, targets, out):
    total = sums[0]
    for i in range(1, sums.shape[0]):
        total = total + sums[i]
    out[...] = total * scale - targets[...]


def delta_kernel(start, place, *refs):
    resid_refs, high_refs, low_refs = refs[:4], refs[4:8], refs[8:12]
    delta, *mine, resid_high, resid_low, high, low = refs[12:]
    quarter = resid_refs[0].shape[0]
    outputs, here = delta.shape
    columns = pl.ds(start, here)
    x, y_lo, y_hi, z = place[0], place[1], place[2], place[3]
    for way in range(4):
        resid = resid_refs[way]
        rows = pl.ds(way * quarter, quarter)
        resid_high[rows, :], resid_low[rows, :] = parts(resid[...])
        high[rows, :], low[rows, :] = high_refs[way][:, columns], low_refs[way][:, columns]
        for out in mine:
            own = out.shape[0] // 8
            for half in range(2):
                source = (half * 4 + y_hi * 2 + z % 2) * (quarter // 8) + z // 2 * own
                target = ((y_lo + way // 2) % 2 * RING + 2 * half + (x + way) % 2) * own
                for row in range(own):
                    out[pl.ds(target + row, 1), :] = resid[pl.ds(source + row, 1), :][:, :outputs]
    found = product((high[...], low[...]), (resid_high[...], resid_low[...]), ((0,), (0,)))
    delta[...] = found.T[:outputs]


def update_kernel(factor, place, weights, own_delta, other_delta, mine, theirs, out, residual):
    step = pl.program_id(0)

    @pl.when(step == 0)
    def _():
        rows = mine.shape[0]
        core = place[4]
        residual[pl.ds(pl.multiple_of(core * rows, 8), rows), :] = mine[...]
        residual[pl.ds(pl.multiple_of((1 - core) * rows, 8), rows), :] = theirs[...]

    rows = pl.ds(pl.multiple_of(step * out.shape[0], 8), out.shape[0])
    out[...] = weights[rows, :] - factor * (own_delta[rows, :] + other_delta[rows, :])


def update(factor, steps, place, weights, own_delta, other_delta, mine, theirs):
    outputs, here = weights.shape
    block = 2 * mine.shape[0]
    return pl.pallas_call(
        functools.partial(update_kernel, factor),
        grid=(steps,),
        in_specs=[pl.BlockSpec(memory_space=pltpu.SMEM)]
        + [pl.BlockSpec(memory_space=pltpu.VMEM)] * 5,
        out_specs=[
            pl.BlockSpec((outputs // steps, here), lambda i: (i, 0)),
            pl.BlockSpec((block, outputs), lambda i: (0, 0)),
        ],
        out_shape=[
            jax.ShapeDtypeStruct((outputs, here), jnp.float32),
            jax.ShapeDtypeStruct((block, outputs), jnp.float32),
        ],
        compiler_params=pltpu.CompilerParams(vmem_limit_bytes=VMEM_BYTES),
    )(place, weights, own_delta, other_delta, mine, theirs)


def call(kernel, outs, *operands, scratch=(), scalars=0, products=0):
    return pl.pallas_call(
        kernel,
        in_specs=[pl.BlockSpec(memory_space=pltpu.SMEM)] * scalars
        + [pl.BlockSpec(memory_space=pltpu.VMEM)] * (len(operands) - scalars),
        out_shape=[jax.ShapeDtypeStruct(shape, dtype) for shape, dtype in outs],
        scratch_shapes=[pltpu.VMEM(shape, dtype) for shape, dtype in scratch],
        compiler_params=pltpu.CompilerParams(vmem_limit_bytes=VMEM_BYTES),
        cost_estimate=pl.CostEstimate(
            flops=2 * products, bytes_accessed=VMEM_BYTES // 8, transcendentals=0
        ),
    )(*operands)


def per_device(batch_index, train_features, train_labels, centers, weights):
    block = batch_index.shape[0]
    features = centers.shape[1]
    outputs = weights.shape[1]
    here = centers.shape[0]
    devices = math.prod(SIZES)
    batch = block * LEVELS * 2
    scale = 1.0 / math.sqrt(here * devices)
    x, core, z = lax.axis_index("x"), lax.axis_index("core"), lax.axis_index("z")
    y_lo, y_hi = lax.axis_index("y_lo"), lax.axis_index("y_hi")
    own = block // (2 * RING * 2)
    start = (core * 2 * RING + y_lo * RING + x) * own
    index = lax.dynamic_slice_in_dim(batch_index, start, own, 0)
    lanes = -(-outputs // LANE) * LANE
    half_block = block // 2
    order = jnp.arange(half_block)
    high, odd, far, row = order // (4 * own), order // (2 * own) % 2, order // own % 2, order % own
    turn = odd ^ z % 2
    wanted = ((y_lo ^ y_hi ^ high ^ turn) * RING + 2 * far + (x % 2 ^ turn)) * own + row
    match = (core * half_block + wanted)[:, None] == jnp.arange(block)[None, :]
    wanted_index = jnp.sum(jnp.where(match, batch_index[None, :], 0), axis=1)
    rows = pick(train_features, wanted_index)
    place = jnp.stack([x, y_lo, y_hi, z, core]).astype(jnp.int32)
    rows, place, index, own_centers, own_weights = lax.optimization_barrier(
        (rows, place, index, centers, weights)
    )
    other_centers, other_weights = permute(own_centers, SWAP), permute(own_weights, SWAP)
    sent = jnp.broadcast_to(
        rows.reshape(2, 1, 2, 2 * own, features), (2, LEVELS // 2, 2, 2 * own, features)
    )
    found = exchange(sent.reshape(-1, features), LINES)
    found, own_centers, own_weights, other_centers, other_weights, train_labels = (
        lax.optimization_barrier(
            (found, own_centers, own_weights, other_centers, other_weights, train_labels)
        )
    )
    (column,) = call(
        functools.partial(order_kernel, own), ((found.shape, jnp.float32),), found
    )
    column_rows = LEVELS // 2 * own
    quarter = found.shape[0]
    pair = 2 * here
    *held, targets = call(
        functools.partial(prepare_kernel, own),
        (
            ((features, pair), jnp.bfloat16),
            ((features, pair), jnp.bfloat16),
            ((1, pair), jnp.float32),
            ((pair, lanes), jnp.bfloat16),
            ((pair, lanes), jnp.bfloat16),
            ((column_rows, lanes), jnp.float32),
        ),
        index,
        place,
        own_centers,
        other_centers,
        own_weights.T,
        other_weights.T,
        train_labels.T,
        scratch=(((train_labels.shape[0], lanes), jnp.float32),),
        scalars=2,
    )

    def quarter_of(part):
        return call(
            quarter_kernel,
            (
                ((quarter, lanes), jnp.float32),
                ((quarter, pair), jnp.bfloat16),
                ((quarter, pair), jnp.bfloat16),
            ),
            part,
            *held,
            products=3 * quarter * pair * (features + lanes),
        )

    first_rows, *later = quarters(column)
    done = [quarter_of(first_rows)]
    value = done[0][0]
    sums = []
    for way, part in zip(WAYS, later):
        part, value = lax.optimization_barrier((part, value))
        done.append(quarter_of(part))
        sums.append(permute(done[way][0], swap_pairs(way)))
    for found in sums:
        value = value + found
    sums = exchange(value, PLANES).reshape(len(PLANES[0]), column_rows, lanes)
    (value,) = call(
        functools.partial(plane_kernel, scale), (((column_rows, lanes), jnp.float32),), sums, targets
    )
    opposite, up, down = (permute(value, along_z(step)) for step in (4, 2, -2))
    resid_list = quarters(spread((value + opposite) + (up + down), PLANES))

    def delta_of(start, *outs):
        return call(
            functools.partial(delta_kernel, start),
            (((outputs, here), jnp.float32), *outs),
            place,
            *resid_list,
            *(part[1] for part in done),
            *(part[2] for part in done),
            scratch=(((4 * quarter, lanes), jnp.bfloat16),) * 2
            + (((4 * quarter, here), jnp.bfloat16),) * 2,
            scalars=1,
            products=3 * 4 * quarter * here * lanes,
        )

    first, mine = delta_of(here, ((half_block, outputs), jnp.float32))
    received, theirs = permute(first, SWAP), permute(mine, SWAP)
    *resid_list, first = lax.optimization_barrier((*resid_list, first))
    (second,) = delta_of(0)
    new_weights, residual = update(
        step_size / batch, 5, place, weights.T, second, received, mine, theirs
    )
    return (new_weights.T, residual)


def solution(mesh):
    split = Mesh(mesh.devices.reshape(SIZES), AXES)
    placed = (
        P(NARROW),
        P(NARROW, None),
        P(NARROW, None),
        P(WIDE_NARROW, None),
        P(WIDE_NARROW, None),
    )
    return jax.shard_map(
        per_device,
        mesh=split,
        in_specs=placed,
        out_specs=(P(WIDE_NARROW, None), P(NARROW, None)),
        check_vma=False,
    )
```

```python
import functools
import math

import jax
import jax.numpy as jnp
from jax import lax
from jax.experimental import pallas as pl
from jax.experimental.pallas import tpu as pltpu
from jax.sharding import Mesh
from jax.sharding import PartitionSpec as P

AXES = ("y_lo", "x", "core", "z", "y_hi")
SIZES = (2, 4, 2, 8, 2)
WIDE_NARROW = AXES
NARROW = ("z", "y_hi")
RING = 4
LEVELS = 8
LANE = 128
WAYS = (1, 2, 3)

VMEM_BYTES = 16 * 1024 * 1024

step_size = 1.0


def position(x, y, z, core):
    x, y = x % RING, y % RING
    return (((y % 2 * RING + x) * 2 + core) * LEVELS + z) * 2 + y // 2


def everywhere():
    return [
        (x, y, z, core)
        for x in range(RING)
        for y in range(RING)
        for z in range(LEVELS)
        for core in range(2)
    ]


def beside(place, core):
    return place + 1 if place % 2 == core else place - 1


def neighbour(x, y, z, core, way):
    if way == 1:
        x = beside(x, core)
    elif way == 2:
        y = beside(y, core)
    elif way == 3:
        z = beside(z, core)
    return position(x, y, z % LEVELS, core)


def swap_pairs(way):
    return [(position(*device), neighbour(*device, way)) for device in everywhere()]


SWAP = [(position(x, y, z, core), position(x, y, z, 1 - core)) for x, y, z, core in everywhere()]
PLANES = [
    [
        position(2 * i + (low ^ odd), 2 * k + (high ^ odd), 2 * level + odd, core)
        for i in range(2)
        for k in range(2)
        for odd in range(2)
    ]
    for low in range(2)
    for high in range(2)
    for level in range(LEVELS // 2)
    for core in range(2)
]
LINES = [
    [
        position(x, first if high == 0 else RING - 1 - first, z, core)
        for high in range(2)
        for z in range(LEVELS)
    ]
    for x in range(RING)
    for first in range(2)
    for core in range(2)
]


def along_z(step):
    return [
        (position(x, y, z, core), position(x, y, (z + step) % LEVELS, core))
        for x, y, z, core in everywhere()
    ]


def permute(array, pairs):
    return lax.ppermute(array, AXES, pairs)


def exchange(array, groups):
    return lax.all_to_all(array, AXES, 0, 0, axis_index_groups=groups, tiled=True)


def spread(array, groups):
    count = len(groups[0])
    copies = jnp.broadcast_to(array[None], (count,) + array.shape)
    return exchange(copies.reshape((-1,) + array.shape[1:]), groups)


def quarters(own):
    return [own] + [permute(own, swap_pairs(way)) for way in WAYS]


def pick(array, index):
    return array.at[index].get(mode="promise_in_bounds")


def parts(array):
    high = array.astype(jnp.bfloat16)
    return high, (array - high.astype(jnp.float32)).astype(jnp.bfloat16)


def product(left, right, contract):
    def one(a, b):
        return lax.dot_general(
            a, b, (contract, ((), ())), preferred_element_type=jnp.float32
        )

    return one(left[0], right[0]) + (one(left[0], right[1]) + one(left[1], right[0]))


def prepare_kernel(
    own,
    index,
    place,
    own_centers,
    other_centers,
    own_weights,
    other_weights,
    labels,
    high,
    low,
    center_sq,
    value_high,
    value_low,
    targets,
    turned_labels,
):
    here = own_centers.shape[0]
    outputs, lanes = own_weights.shape[0], value_high.shape[1]

    def padded(array):
        zeros = jnp.zeros((lanes - outputs, array.shape[1]), jnp.float32)
        return jnp.concatenate([array, zeros], axis=0).T

    for i, (centers, weights) in enumerate(
        ((own_centers, own_weights), (other_centers, other_weights))
    ):
        columns = pl.ds(i * here, here)
        turned = centers[...].T
        center_sq[:, columns] = jnp.sum(turned * turned, axis=0, keepdims=True)
        high[:, columns], low[:, columns] = parts(turned)
        value_high[columns, :], value_low[columns, :] = parts(padded(weights[...]))
    turned_labels[...] = padded(labels[...])
    targets[...] = jnp.zeros_like(targets)
    start = place[3] // 2 * own
    for row in range(own):
        targets[pl.ds(start + row, 1), :] = turned_labels[pl.ds(index[row], 1), :]


def quarter_kernel(
    rows, centers_high, centers_low, center_sq, weights_high, weights_low, value, high, low
):
    features = rows.shape[1]
    part = rows[...]
    row_sq = jnp.sum(part * part, axis=1, keepdims=True)
    inner = stacked_product(parts(part), (centers_high[...], centers_low[...]))
    kernel = parts(jnp.exp((2.0 * features - row_sq - center_sq[...] + 2.0 * inner) / 128.0))
    high[...], low[...] = kernel
    value[...] = stacked_product(kernel, (weights_high[...], weights_low[...]))


def stacked_product(left, right):
    def one(a, b):
        return jnp.dot(a, b, preferred_element_type=jnp.float32)

    rows = left[0].shape[0]
    both = one(jnp.concatenate(left, axis=0), right[0])
    return both[:rows] + (one(left[0], right[1]) + both[rows:])


def order_kernel(own, found, out):
    levels = LEVELS // 2
    for i in range(2):
        for k in range(2):
            for odd in range(2):
                for level in range(levels):
                    source = (((k * levels + level) * 2 + odd) * 2 + i) * own
                    target = (((i * 2 + k) * 2 + odd) * levels + level) * own
                    out[target : target + own, :] = found[source : source + own, :]


def plane_kernel(scale, sums, targets, out):
    total = sums[0]
    for i in range(1, sums.shape[0]):
        total = total + sums[i]
    out[...] = total * scale - targets[...]


def delta_kernel(start, factor, place, *refs):
    resid_refs, high_refs, low_refs = refs[:4], refs[4:8], refs[8:12]
    weights, refs = (refs[12:13], refs[13:]) if factor else ((), refs[12:])
    delta, *mine, resid_high, resid_low, high, low = refs
    quarter = resid_refs[0].shape[0]
    outputs, here = delta.shape
    columns = pl.ds(start, here)
    x, y_lo, y_hi, z = place[0], place[1], place[2], place[3]
    for way in range(4):
        resid = resid_refs[way]
        rows = pl.ds(way * quarter, quarter)
        resid_high[rows, :], resid_low[rows, :] = parts(resid[...])
        high[rows, :], low[rows, :] = high_refs[way][:, columns], low_refs[way][:, columns]
        for out in mine:
            own = out.shape[0] // 8
            for half in range(2):
                source = (half * 4 + y_hi * 2 + z % 2) * (quarter // 8) + z // 2 * own
                target = ((y_lo + way // 2) % 2 * RING + 2 * half + (x + way) % 2) * own
                for row in range(own):
                    out[pl.ds(target + row, 1), :] = resid[pl.ds(source + row, 1), :][:, :outputs]
    found = product((high[...], low[...]), (resid_high[...], resid_low[...]), ((0,), (0,)))
    delta[...] = weights[0][...] - factor * found.T[:outputs] if weights else found.T[:outputs]


def update_kernel(factor, place, partly, other_delta, mine, theirs, out, residual):
    rows = mine.shape[0]
    core = place[4]
    residual[pl.ds(pl.multiple_of(core * rows, 8), rows), :] = mine[...]
    residual[pl.ds(pl.multiple_of((1 - core) * rows, 8), rows), :] = theirs[...]
    out[...] = partly[...] - factor * other_delta[...]


def call(kernel, outs, *operands, scratch=(), scalars=0, products=0):
    return pl.pallas_call(
        kernel,
        in_specs=[pl.BlockSpec(memory_space=pltpu.SMEM)] * scalars
        + [pl.BlockSpec(memory_space=pltpu.VMEM)] * (len(operands) - scalars),
        out_shape=[jax.ShapeDtypeStruct(shape, dtype) for shape, dtype in outs],
        scratch_shapes=[pltpu.VMEM(shape, dtype) for shape, dtype in scratch],
        compiler_params=pltpu.CompilerParams(vmem_limit_bytes=VMEM_BYTES),
        cost_estimate=pl.CostEstimate(
            flops=2 * products, bytes_accessed=VMEM_BYTES // 8, transcendentals=0
        ),
    )(*operands)


def per_device(batch_index, train_features, train_labels, centers, weights):
    block = batch_index.shape[0]
    features = centers.shape[1]
    outputs = weights.shape[1]
    here = centers.shape[0]
    devices = math.prod(SIZES)
    batch = block * LEVELS * 2
    scale = 1.0 / math.sqrt(here * devices)
    x, core, z = lax.axis_index("x"), lax.axis_index("core"), lax.axis_index("z")
    y_lo, y_hi = lax.axis_index("y_lo"), lax.axis_index("y_hi")
    own = block // (2 * RING * 2)
    start = (core * 2 * RING + y_lo * RING + x) * own
    index = lax.dynamic_slice_in_dim(batch_index, start, own, 0)
    lanes = -(-outputs // LANE) * LANE
    half_block = block // 2
    order = jnp.arange(half_block)
    high, odd, far, row = order // (4 * own), order // (2 * own) % 2, order // own % 2, order % own
    turn = odd ^ z % 2
    wanted = ((y_lo ^ y_hi ^ high ^ turn) * RING + 2 * far + (x % 2 ^ turn)) * own + row
    match = (core * half_block + wanted)[:, None] == jnp.arange(block)[None, :]
    wanted_index = jnp.sum(jnp.where(match, batch_index[None, :], 0), axis=1)
    rows = pick(train_features, wanted_index)
    place = jnp.stack([x, y_lo, y_hi, z, core]).astype(jnp.int32)
    rows, place, index, own_centers, own_weights = lax.optimization_barrier(
        (rows, place, index, centers, weights)
    )
    other_centers, other_weights = permute(own_centers, SWAP), permute(own_weights, SWAP)
    sent = jnp.broadcast_to(
        rows.reshape(2, 1, 2, 2 * own, features), (2, LEVELS // 2, 2, 2 * own, features)
    )
    found = exchange(sent.reshape(-1, features), LINES)
    found, own_centers, own_weights, other_centers, other_weights, train_labels = (
        lax.optimization_barrier(
            (found, own_centers, own_weights, other_centers, other_weights, train_labels)
        )
    )
    (column,) = call(
        functools.partial(order_kernel, own), ((found.shape, jnp.float32),), found
    )
    column_rows = LEVELS // 2 * own
    quarter = found.shape[0]
    pair = 2 * here
    *held, targets = call(
        functools.partial(prepare_kernel, own),
        (
            ((features, pair), jnp.bfloat16),
            ((features, pair), jnp.bfloat16),
            ((1, pair), jnp.float32),
            ((pair, lanes), jnp.bfloat16),
            ((pair, lanes), jnp.bfloat16),
            ((column_rows, lanes), jnp.float32),
        ),
        index,
        place,
        own_centers,
        other_centers,
        own_weights.T,
        other_weights.T,
        train_labels.T,
        scratch=(((train_labels.shape[0], lanes), jnp.float32),),
        scalars=2,
    )

    def quarter_of(part):
        return call(
            quarter_kernel,
            (
                ((quarter, lanes), jnp.float32),
                ((quarter, pair), jnp.bfloat16),
                ((quarter, pair), jnp.bfloat16),
            ),
            part,
            *held,
            products=3 * quarter * pair * (features + lanes),
        )

    first_rows, *later = quarters(column)
    done = [quarter_of(first_rows)]
    value = done[0][0]
    sums = []
    for way, part in zip(WAYS, later):
        part, value = lax.optimization_barrier((part, value))
        done.append(quarter_of(part))
        sums.append(permute(done[way][0], swap_pairs(way)))
    for found in sums:
        value = value + found
    sums = exchange(value, PLANES).reshape(len(PLANES[0]), column_rows, lanes)
    (value,) = call(
        functools.partial(plane_kernel, scale), (((column_rows, lanes), jnp.float32),), sums, targets
    )
    opposite, up, down = (permute(value, along_z(step)) for step in (4, 2, -2))
    resid_list = quarters(spread((value + opposite) + (up + down), PLANES))

    def delta_of(start, factor, extra, *outs):
        return call(
            functools.partial(delta_kernel, start, factor),
            (((outputs, here), jnp.float32), *outs),
            place,
            *resid_list,
            *(part[1] for part in done),
            *(part[2] for part in done),
            *extra,
            scratch=(((4 * quarter, lanes), jnp.bfloat16),) * 2
            + (((4 * quarter, here), jnp.bfloat16),) * 2,
            scalars=1,
            products=3 * 4 * quarter * here * lanes,
        )

    first, mine = delta_of(here, 0.0, (), ((half_block, outputs), jnp.float32))
    received, theirs = permute(first, SWAP), permute(mine, SWAP)
    *resid_list, first = lax.optimization_barrier((*resid_list, first))
    (partly,) = delta_of(0, step_size / batch, (weights.T,))
    new_weights, residual = call(
        functools.partial(update_kernel, step_size / batch),
        (((outputs, here), jnp.float32), ((block, outputs), jnp.float32)),
        place,
        partly,
        received,
        mine,
        theirs,
        scalars=1,
    )
    return (new_weights.T, residual)


def solution(mesh):
    split = Mesh(mesh.devices.reshape(SIZES), AXES)
    placed = (
        P(NARROW),
        P(NARROW, None),
        P(NARROW, None),
        P(WIDE_NARROW, None),
        P(WIDE_NARROW, None),
    )
    return jax.shard_map(
        per_device,
        mesh=split,
        in_specs=placed,
        out_specs=(P(WIDE_NARROW, None), P(NARROW, None)),
        check_vma=False,
    )
```
